128 devices in a mesh: row: 8 (over x_lo, z), col: 16 (over y, x_hi, core).
Axes of the slice: x: 4 (x_hi: 2, x_lo: 2; x = x_hi * 2 + x_lo), y: 4, z: 4, core: 2. Of those that a mesh axis runs over, the one named last changes fastest.
Arguments:
- examples: bfloat16 [262144, 1024], P(('row', 'col')), may hold values from -20 to 20
- residuals: float32 [262144, 256], P(('row', 'col')), may hold values from -6 to 6
- coefficients: float32 [262144, 256], P(('row', 'col')), may hold values from -0.8 to 0.8
- block_index: int32 [1], replicated, may hold values from 0 to 255
Outputs:
- new_residuals: float32 [262144, 256], P(('row', 'col'))
- new_coefficients: float32 [262144, 256], P(('row', 'col'))
The draws below stay inside these ranges and needn't reach their ends.
All inputs are finite; a program needn't handle non-finite values.
Results may differ from the reference program's by a relative error of at most 0.00035.
Values may be sent and summed in bfloat16 or wider, within the bound.
A program may use at most 128 MiB of HBM per device.

```python
import math
import jax
import jax.numpy as jnp
from jax import lax

FEATURES = 1024
OUTPUTS = 256
BLOCK = 1024
EX_DEV = 2048
EXAMPLES = 262144


def draw_examples(key, part):
    latent_count = 6
    key_latent = jax.random.fold_in(key, 11)
    key_mixing = jax.random.fold_in(key, 12)
    key_noise = jax.random.fold_in(key, 13)
    mixing = jax.random.normal(key_mixing, (latent_count, FEATURES), jnp.float32) / math.sqrt(latent_count)
    spread = math.sqrt(2.0 * latent_count)
    latent = jax.random.normal(key_latent, (EXAMPLES, latent_count), jnp.float32)
    noise = 0.5 * jax.random.normal(key_noise, (EXAMPLES, FEATURES), jnp.float32)
    values = spread * jnp.dot(latent, mixing, precision=lax.Precision.HIGHEST) + noise
    return jnp.clip(values, -20.0, 20.0).astype(jnp.bfloat16)


def block_scale(stream_key, shape, split, least, high):
    factor_of, own = 1.0, jax.random.fold_in(stream_key, 6)
    for axis_at, blocks in split:
        heights = jnp.exp(jax.random.uniform(jax.random.fold_in(own, axis_at), (blocks,), jnp.float32, least / len(split), high / len(split)))
        factor_of = factor_of * jnp.repeat(heights, shape[axis_at] // blocks).reshape([-1 if axis == axis_at else 1 for axis in range(len(shape))])
    return factor_of


def normal_values(stream_key, extent, scale, limit, cuts=(), kind=jnp.bfloat16):
    result = jax.random.normal(stream_key, extent, jnp.float32) * scale
    if len(cuts) > 0:
        result = block_scale(stream_key, extent, cuts, -0.22, 0.18) * result
    return jnp.clip(result, min=-limit, max=limit).astype(kind)


def setup_inputs(seed: int = 0) -> dict:
    key_of = jax.random.split(jax.random.key(seed), 5)
    return {
        "examples": draw_examples(jax.random.fold_in(key_of[4], 71), 0),
        "residuals": normal_values(key_of[1], (EXAMPLES, OUTPUTS), 1.0, 6.0, ((0, 128),), jnp.float32),
        "coefficients": normal_values(key_of[2], (EXAMPLES, OUTPUTS), 0.1, 0.8, ((0, 128),), jnp.float32),
        "block_index": jax.random.randint(key_of[3], (1,), 0, EXAMPLES // BLOCK).astype(jnp.int32),
    }


ridge = 0.001
width_factor = 0.5

def reference(examples, residuals, coefficients, block_index):
    chosen = block_index[0].astype(jnp.int32)
    start = (chosen * BLOCK).astype(jnp.int32)
    block_rows = lax.dynamic_slice_in_dim(examples, start, BLOCK, 0)
    block_coef = lax.dynamic_slice_in_dim(coefficients, start, BLOCK, 0)
    sq_block = jnp.sum(jnp.square(block_rows.astype(jnp.float32)), axis=1)
    shards = EXAMPLES // EX_DEV
    grouped = examples.reshape(shards, EX_DEV, FEATURES)
    grouped_res = residuals.reshape(shards, EX_DEV, OUTPUTS)

    def one_shard(carry, pair):
        rows, res = pair
        sq_rows = jnp.sum(jnp.square(rows.astype(jnp.float32)), axis=1)
        inner = jnp.dot(rows.astype(jnp.float32), block_rows.T.astype(jnp.float32), preferred_element_type=jnp.float32)
        kernel = jnp.exp(-width_factor * (sq_rows[:, None] + sq_block[None, :] - 2.0 * inner) / FEATURES).astype(jnp.bfloat16)
        residual_low = res.astype(jnp.bfloat16)
        grad_part = jnp.dot(kernel.T.astype(jnp.float32), residual_low.astype(jnp.float32), preferred_element_type=jnp.float32)
        gram_part = jnp.dot(kernel.T.astype(jnp.float32), kernel.astype(jnp.float32), preferred_element_type=jnp.float32)
        return ((carry[0] + grad_part, carry[1] + gram_part), kernel)
    init = (jnp.zeros((BLOCK, OUTPUTS), jnp.float32), jnp.zeros((BLOCK, BLOCK), jnp.float32))
    (grad, gram), kernels = lax.scan(one_shard, init, (grouped, grouped_res))
    grad = grad - EXAMPLES * ridge * block_coef
    system = gram / EXAMPLES + ridge * jnp.eye(BLOCK, dtype=jnp.float32)
    factor = jnp.linalg.cholesky(system)
    update = jax.scipy.linalg.cho_solve((factor, True), grad / EXAMPLES)
    update_low = update.astype(jnp.bfloat16)

    def apply_shard(kernel):
        return jnp.dot(kernel.astype(jnp.float32), update_low.astype(jnp.float32), preferred_element_type=jnp.float32)
    change = lax.map(apply_shard, kernels).reshape(EXAMPLES, OUTPUTS)
    new_residuals = residuals - change
    new_coefficients = lax.dynamic_update_slice_in_dim(coefficients, block_coef + update, start, 0)
    return (new_residuals, new_coefficients)
```

```python
import functools
import jax
import jax.numpy as jnp
from jax import lax
from jax.experimental import pallas as pl
from jax.experimental.pallas import tpu as pltpu
from jax.sharding import PartitionSpec as P

BLOCK = 1024


ridge = 0.001
width_factor = 0.5

HI = lax.Precision.HIGHEST
NB = 128

def dot(a, b, ca, cb):
    return lax.dot_general(a, b, (((ca,), (cb,)), ((), ())), precision=HI, preferred_element_type=jnp.float32)

def split3(v):
    h = v.astype(jnp.bfloat16).astype(jnp.float32)
    r = v - h
    m = r.astype(jnp.bfloat16).astype(jnp.float32)
    return h, m, r - m

def factor(M):
    sub = lax.broadcasted_iota(jnp.int32, (8, 128), 0)
    sub2 = lax.broadcasted_iota(jnp.int32, (8, 256), 0)
    lane = lax.broadcasted_iota(jnp.int32, (8, 128), 1)
    for q in range(16):
        r0 = 8 * q
        look = q < 15
        top = M[r0:r0 + 8, :]
        ct = [jnp.broadcast_to(top[:, r0 + j:r0 + j + 1], (8, 128)) for j in range(8)]
        if look:
            bot = M[r0 + 8:r0 + 16, :]
            cb = [jnp.broadcast_to(bot[:, r0 + j:r0 + j + 1], (8, 128)) for j in range(8)]
        for j in range(8):
            r = lax.rsqrt(ct[j][j:j + 1, :])
            r2 = jnp.concatenate([r, r], axis=1)
            row = top[j:j + 1, :] * r2
            mt = jnp.where(sub > j, ct[j] * r, 0.0)
            mt2 = jnp.concatenate([mt, mt], axis=1)
            rows_k = {k: ct[k][j:j + 1, :] * r for k in range(j + 1, 8)}
            top = jnp.where(sub2 == j, row, top - mt2 * row)
            for k in range(j + 1, 8):
                ct[k] = ct[k] - mt * rows_k[k]
            if look:
                mb = cb[j] * r
                mb2 = jnp.concatenate([mb, mb], axis=1)
                bot = bot - mb2 * row
                for k in range(j + 1, 8):
                    cb[k] = cb[k] - mb * rows_k[k]
        M[r0:r0 + 8, :] = top
        if look:
            M[r0 + 8:r0 + 16, :] = bot
        if q < 14:
            h, m, l = split3(top)
            keep = lane >= r0 + 16
            hl, ml, ll = [jnp.where(keep, v[:, :128], 0.0) for v in (h, m, l)]
            lhs = jnp.concatenate([hl, hl, ml, hl, ml, ll], axis=0).astype(jnp.bfloat16)
            rhs = jnp.concatenate([h, m, h, l, m, h], axis=0).astype(jnp.bfloat16)
            res = lax.dot_general(lhs, rhs, (((0,), (0,)), ((), ())), preferred_element_type=jnp.float32)
            M[r0 + 16:, :] = M[r0 + 16:, :] - res[r0 + 16:, :]

def solve_kernel(scale, ridge, gram_ref, grad_ref, upd_ref, low_ref, S, G, M, W):
    n = gram_ref.shape[0]
    nb = n // NB
    eye = (lax.broadcasted_iota(jnp.int32, (NB, NB), 0) == lax.broadcasted_iota(jnp.int32, (NB, NB), 1)).astype(jnp.float32)
    S[...] = gram_ref[...] * scale
    G[...] = grad_ref[...] * scale
    for k in range(nb):
        a, b = k * NB, (k + 1) * NB
        M[:, :NB] = S[a:b, a:b] + ridge * eye
        M[:, NB:] = eye
        factor(M)
        w = M[:, NB:]
        W[a:b, :] = w
        G[a:b, :] = dot(w, G[a:b, :], 1, 0)
        if k < nb - 1:
            u = dot(w, S[a:b, b:], 1, 0)
            l = dot(S[b:, a:b], w, 1, 1)
            S[a:b, b:] = u
            S[b:, b:] = S[b:, b:] - dot(l, u, 1, 0)
            G[b:, :] = G[b:, :] - dot(l, G[a:b, :], 1, 0)
    for k in reversed(range(nb)):
        a, b = k * NB, (k + 1) * NB
        y = G[a:b, :]
        if k < nb - 1:
            y = y - dot(S[a:b, b:], G[b:, :], 1, 0)
        G[a:b, :] = dot(W[a:b, :], y, 0, 0)
    upd_ref[...] = G[...]
    low_ref[...] = G[...].astype(jnp.bfloat16)

def solve(gram, grad, total, ridge):
    n, o = grad.shape
    return pl.pallas_call(
        functools.partial(solve_kernel, 1.0 / total, ridge),
        out_shape=(jax.ShapeDtypeStruct((n, o), jnp.float32), jax.ShapeDtypeStruct((n, o), jnp.bfloat16)),
        in_specs=[pl.BlockSpec(memory_space=pltpu.VMEM)] * 2,
        out_specs=[pl.BlockSpec(memory_space=pltpu.VMEM)] * 2,
        scratch_shapes=[pltpu.VMEM((n, n), jnp.float32), pltpu.VMEM((n, o), jnp.float32), pltpu.VMEM((NB, 2 * NB), jnp.float32), pltpu.VMEM((n, NB), jnp.float32)],
        compiler_params=pltpu.CompilerParams(vmem_limit_bytes=48 * 2**20),
        name="solve_block",
    )(gram, grad)


def spread(value, axis, source):
    kept = jnp.where(lax.axis_index(axis) == source, value, 0).astype(value.dtype)
    return lax.psum(kept, axis)


def body(examples, residuals, coefficients, block_index):
    rows_here = examples.shape[0]
    features = examples.shape[1]
    per_device = rows_here // BLOCK
    devices_all = lax.axis_size(("row", "col"))
    total_examples = rows_here * devices_all
    chosen = block_index[0]
    owner_rank = chosen // per_device
    offset = chosen % per_device * BLOCK
    my_rank = lax.axis_index(("row", "col"))
    is_owner = owner_rank == my_rank
    my_block = lax.dynamic_slice_in_dim(examples, offset, BLOCK, 0)
    block_rows = spread(my_block, ("row", "col"), owner_rank)
    sq_rows = jnp.sum(jnp.square(examples.astype(jnp.float32)), axis=1)
    sq_block = jnp.sum(jnp.square(block_rows.astype(jnp.float32)), axis=1)
    inner = lax.dot_general(
        examples, block_rows, (((1,), (1,)), ((), ())), preferred_element_type=jnp.float32
    )
    kernel = jnp.exp(
        -width_factor * (sq_rows[:, None] + sq_block[None, :] - 2.0 * inner) / features
    ).astype(jnp.bfloat16)
    residual_low = residuals.astype(jnp.bfloat16)
    grad_part = lax.dot_general(
        kernel, residual_low, (((0,), (0,)), ((), ())), preferred_element_type=jnp.float32
    )
    gram_part = lax.dot_general(
        kernel, kernel, (((0,), (0,)), ((), ())), preferred_element_type=jnp.float32
    )
    own_coef = lax.dynamic_slice_in_dim(coefficients, offset, BLOCK, 0)
    weight_own = jnp.where(is_owner, total_examples * ridge, 0.0).astype(jnp.float32)
    grad_part = grad_part - weight_own * own_coef
    grad, gram_sum = lax.psum((grad_part, gram_part), ("row", "col"))
    update, update_low = solve(gram_sum, grad, total_examples, ridge)
    new_residuals = residuals - jnp.dot(kernel, update_low, preferred_element_type=jnp.float32)
    updated = lax.dynamic_update_slice_in_dim(coefficients, own_coef + update, offset, 0)
    new_coefficients = jnp.where(is_owner, updated, coefficients)
    return (new_residuals, new_coefficients)


def solution(mesh):
    in_specs = (P(("row", "col"), None), P(("row", "col"), None), P(("row", "col"), None), P())
    out_specs = (P(("row", "col"), None), P(("row", "col"), None))
    return jax.shard_map(body, mesh=mesh, in_specs=in_specs, out_specs=out_specs, check_vma=False)
```

```python
import functools
import jax
import jax.numpy as jnp
from jax import lax
from jax.experimental import pallas as pl
from jax.experimental.pallas import tpu as pltpu
from jax.sharding import PartitionSpec as P

BLOCK = 1024


ridge = 0.001
width_factor = 0.5


BLOCK_PARTS = ((0, 512, 0, 384), (0, 512, 384, 384), (0, 512, 768, 256))
SUM_PARTS = ((0, 1152, 0, 128), (1152, 1152, 0, 128), (2304, 1280, 0, 128))
AXES = ("x", "y", "z")

def place():
    row, col = lax.axis_index("row"), lax.axis_index("col")
    return {"x": (col // 2) % 2 * 2 + row // 4, "y": col // 4, "z": row % 4, "core": col % 2}

def device(at):
    return (at["x"] % 2 * 4 + at["z"], at["y"] * 4 + at["x"] // 2 * 2 + at["core"])

def shifted(at, axis, by):
    size = 2 if axis == "core" else 4
    return device({**at, axis: (at[axis] + by) % size})

def sum_kernel(parts, unit, x_ref, out_ref, theirs, acc, slot1, slot2, slot3, core_sems, ring_sems):
    at = place()
    half = x_ref.shape[0] // 2
    barrier = pltpu.get_barrier_semaphore()
    peers = [("core", 1)] + [(a, o) for a in AXES for o in (1, 2, 3)]
    for axis, by in peers:
        pl.semaphore_signal(barrier, inc=1, device_id=shifted(at, axis, by), device_id_type=pl.DeviceIdType.MESH)
    pl.semaphore_wait(barrier, len(peers))
    sent = []

    def send(src, dst, sems, who):
        copy = pltpu.make_async_remote_copy(src_ref=src, dst_ref=dst, send_sem=sems.at[0], recv_sem=sems.at[1],
                                            device_id=who, device_id_type=pl.DeviceIdType.MESH)
        copy.start()
        sent.append(copy)
        return copy

    mine, other = at["core"] * half, (1 - at["core"]) * half
    orders = [tuple(AXES[(p + i) % 3] for i in range(3)) for p in range(len(parts))]

    def rows(start, n, c0, cn):
        return (pl.ds(pl.multiple_of(start, unit), n), pl.ds(c0, cn))

    def core_send(p, source, base, target, tbase, k):
        r, n, c0, cn = parts[p]
        return send(source.at[rows(base + r, n, c0, cn)], target.at[rows(tbase + r, n, c0, cn)],
                    core_sems.at[k, p], shifted(at, "core", 1))

    P = range(len(parts))
    pending = [core_send(p, x_ref, other, theirs, 0, 0) for p in P]
    nxt = []
    for p in P:
        r, n, c0, cn = parts[p]
        pending[p].wait_recv()
        acc[rows(r, n, c0, cn)] = x_ref[rows(mine + r, n, c0, cn)] + theirs[rows(r, n, c0, cn)]
        q = n // 4
        a = orders[p][0]
        nxt.append([send(acc.at[rows(r + (at[a] + o) % 4 * q, q, c0, cn)], slot1.at[o - 1, pl.ds(r // 4, q), pl.ds(c0, cn)],
                         ring_sems.at[0, p, o - 1], shifted(at, a, o)) for o in (1, 2, 3)])
    pending, nxt = nxt, []
    begin = []
    for p in P:
        r, n, c0, cn = parts[p]
        for c in pending[p]:
            c.wait_recv()
        q, s = n // 4, n // 16
        a, b = orders[p][:2]
        start = r + at[a] * q
        begin.append(start)
        sl = lambda o: slot1[o - 1, pl.ds(r // 4, q), pl.ds(c0, cn)]
        acc[rows(start, q, c0, cn)] = (acc[rows(start, q, c0, cn)] + sl(2)) + (sl(1) + sl(3))
        nxt.append([send(acc.at[rows(start + (at[b] + o) % 4 * s, s, c0, cn)], slot2.at[o - 1, pl.ds(r // 16, s), pl.ds(c0, cn)],
                         ring_sems.at[1, p, o - 1], shifted(at, b, o)) for o in (1, 2, 3)])
    pending, nxt = nxt, []
    fine = []
    for p in P:
        r, n, c0, cn = parts[p]
        for c in pending[p]:
            c.wait_recv()
        s = n // 16
        b, d = orders[p][1:]
        start = begin[p] + at[b] * s
        fine.append(start)
        sl = lambda o: slot2[o - 1, pl.ds(r // 16, s), pl.ds(c0, cn)]
        acc[rows(start, s, c0, cn)] = (acc[rows(start, s, c0, cn)] + sl(2)) + (sl(1) + sl(3))
        nxt.append([send(acc.at[rows(start, s, c0, cn)], slot3.at[o - 1, pl.ds(r // 16, s), pl.ds(c0, cn)],
                         ring_sems.at[2, p, o - 1], shifted(at, d, o)) for o in (1, 2, 3)])
    pending, nxt = nxt, []
    for p in P:
        r, n, c0, cn = parts[p]
        for c in pending[p]:
            c.wait_recv()
        s = n // 16
        b = orders[p][1]
        sl = lambda o: slot3[o - 1, pl.ds(r // 16, s), pl.ds(c0, cn)]
        out_ref[rows(mine + fine[p], s, c0, cn)] = (acc[rows(fine[p], s, c0, cn)] + sl(2)) + (sl(1) + sl(3))
        here = out_ref.at[rows(mine + fine[p], s, c0, cn)]
        nxt.append([send(here, here, ring_sems.at[3, p, o - 1], shifted(at, b, o)) for o in (1, 2, 3)])
    pending, nxt = nxt, []
    for p in P:
        r, n, c0, cn = parts[p]
        for c in pending[p]:
            c.wait_recv()
        q = n // 4
        a = orders[p][0]
        here = out_ref.at[rows(mine + begin[p], q, c0, cn)]
        nxt.append([send(here, here, ring_sems.at[4, p, o - 1], shifted(at, a, o)) for o in (1, 2, 3)])
    pending, nxt = nxt, []
    for p in P:
        for c in pending[p]:
            c.wait_recv()
        nxt.append(core_send(p, out_ref, mine, out_ref, mine, 1))
    for p in P:
        nxt[p].wait_recv()
    for copy in sent:
        copy.wait_send()

def all_sum(x, parts, collective_id, name):
    n, w = x.shape
    half = n // 2
    unit = 16 if x.dtype == jnp.bfloat16 else 8
    dt = x.dtype
    return pl.pallas_call(
        functools.partial(sum_kernel, parts, unit),
        out_shape=jax.ShapeDtypeStruct(x.shape, dt),
        in_specs=[pl.BlockSpec(memory_space=pltpu.VMEM)],
        out_specs=pl.BlockSpec(memory_space=pltpu.VMEM),
        scratch_shapes=[
            pltpu.VMEM((half, w), dt), pltpu.VMEM((half, w), dt),
            pltpu.VMEM((3, half // 4, w), dt), pltpu.VMEM((3, half // 16, w), dt), pltpu.VMEM((3, half // 16, w), dt),
            pltpu.SemaphoreType.DMA((2, 3, 2)), pltpu.SemaphoreType.DMA((5, 3, 3, 2)),
        ],
        compiler_params=pltpu.CompilerParams(collective_id=collective_id, has_side_effects=True, vmem_limit_bytes=48 * 2**20),
        name=name,
    )(x)


HI = lax.Precision.HIGHEST
NB = 128

def dot(a, b, ca, cb):
    return lax.dot_general(a, b, (((ca,), (cb,)), ((), ())), precision=HI, preferred_element_type=jnp.float32)

def split3(v):
    h = v.astype(jnp.bfloat16).astype(jnp.float32)
    r = v - h
    m = r.astype(jnp.bfloat16).astype(jnp.float32)
    return h, m, r - m

def factor(M):
    sub = lax.broadcasted_iota(jnp.int32, (8, 128), 0)
    sub2 = lax.broadcasted_iota(jnp.int32, (8, 256), 0)
    lane = lax.broadcasted_iota(jnp.int32, (8, 128), 1)
    for q in range(16):
        r0 = 8 * q
        look = q < 15
        top = M[r0:r0 + 8, :]
        ct = [jnp.broadcast_to(top[:, r0 + j:r0 + j + 1], (8, 128)) for j in range(8)]
        if look:
            bot = M[r0 + 8:r0 + 16, :]
            cb = [jnp.broadcast_to(bot[:, r0 + j:r0 + j + 1], (8, 128)) for j in range(8)]
        for j in range(8):
            r = lax.rsqrt(ct[j][j:j + 1, :])
            r2 = jnp.concatenate([r, r], axis=1)
            row = top[j:j + 1, :] * r2
            mt = jnp.where(sub > j, ct[j] * r, 0.0)
            mt2 = jnp.concatenate([mt, mt], axis=1)
            rows_k = {k: ct[k][j:j + 1, :] * r for k in range(j + 1, 8)}
            top = jnp.where(sub2 == j, row, top - mt2 * row)
            for k in range(j + 1, 8):
                ct[k] = ct[k] - mt * rows_k[k]
            if look:
                mb = cb[j] * r
                mb2 = jnp.concatenate([mb, mb], axis=1)
                bot = bot - mb2 * row
                for k in range(j + 1, 8):
                    cb[k] = cb[k] - mb * rows_k[k]
        M[r0:r0 + 8, :] = top
        if look:
            M[r0 + 8:r0 + 16, :] = bot
        if q < 14:
            h, m, l = split3(top)
            keep = lane >= r0 + 16
            hl, ml, ll = [jnp.where(keep, v[:, :128], 0.0) for v in (h, m, l)]
            lhs = jnp.concatenate([hl, hl, ml, hl, ml, ll], axis=0).astype(jnp.bfloat16)
            rhs = jnp.concatenate([h, m, h, l, m, h], axis=0).astype(jnp.bfloat16)
            res = lax.dot_general(lhs, rhs, (((0,), (0,)), ((), ())), preferred_element_type=jnp.float32)
            M[r0 + 16:, :] = M[r0 + 16:, :] - res[r0 + 16:, :]

def solve_kernel(scale, ridge, sums_ref, upd_ref, low_ref, S, G, M, W):
    n = S.shape[0]
    nb = n // NB
    eye = (lax.broadcasted_iota(jnp.int32, (NB, NB), 0) == lax.broadcasted_iota(jnp.int32, (NB, NB), 1)).astype(jnp.float32)
    at = 0
    for c in range(0, n, NB):
        depth = c // 256 * 256 + 256
        S[0:depth, c:c + NB] = sums_ref[at:at + depth, :] * scale
        at += depth
    for c in range(0, G.shape[1], NB):
        G[:, c:c + NB] = sums_ref[at:at + n, :] * scale
        at += n
    for k in range(nb):
        a, b = k * NB, (k + 1) * NB
        M[:, :NB] = S[a:b, a:b] + ridge * eye
        M[:, NB:] = eye
        factor(M)
        w = M[:, NB:]
        W[a:b, :] = w
        G[a:b, :] = dot(w, G[a:b, :], 1, 0)
        if k < nb - 1:
            u = dot(w, S[a:b, b:], 1, 0)
            S[a:b, b:] = u
            for i in range(b, n, NB):
                S[i:i + NB, i:] = S[i:i + NB, i:] - dot(u[:, i - b:i - b + NB], u[:, i - b:], 0, 0)
            G[b:, :] = G[b:, :] - dot(u, G[a:b, :], 0, 0)
    for k in reversed(range(nb)):
        a, b = k * NB, (k + 1) * NB
        y = G[a:b, :]
        if k < nb - 1:
            y = y - dot(S[a:b, b:], G[b:, :], 1, 0)
        G[a:b, :] = dot(W[a:b, :], y, 0, 0)
    upd_ref[...] = G[...]
    low_ref[...] = G[...].astype(jnp.bfloat16)

def solve(sums, n, o, total, ridge):
    return pl.pallas_call(
        functools.partial(solve_kernel, 1.0 / total, ridge),
        out_shape=(jax.ShapeDtypeStruct((n, o), jnp.float32), jax.ShapeDtypeStruct((n, o), jnp.bfloat16)),
        in_specs=[pl.BlockSpec(memory_space=pltpu.VMEM)],
        out_specs=[pl.BlockSpec(memory_space=pltpu.VMEM)] * 2,
        scratch_shapes=[pltpu.VMEM((n, n), jnp.float32), pltpu.VMEM((n, o), jnp.float32), pltpu.VMEM((NB, 2 * NB), jnp.float32), pltpu.VMEM((n, NB), jnp.float32)],
        compiler_params=pltpu.CompilerParams(vmem_limit_bytes=48 * 2**20),
        name="solve_block",
    )(sums)


def body(examples, residuals, coefficients, block_index):
    rows_here = examples.shape[0]
    features = examples.shape[1]
    per_device = rows_here // BLOCK
    devices_all = lax.axis_size(("row", "col"))
    total_examples = rows_here * devices_all
    chosen = block_index[0]
    owner_rank = chosen // per_device
    offset = chosen % per_device * BLOCK
    my_rank = lax.axis_index(("row", "col"))
    is_owner = owner_rank == my_rank
    my_block = lax.dynamic_slice_in_dim(examples, offset, BLOCK, 0)
    kept = jnp.where(is_owner, my_block, 0).astype(my_block.dtype)
    block_rows = all_sum(kept, BLOCK_PARTS, 1, "block_spread")
    sq_rows = jnp.sum(jnp.square(examples.astype(jnp.float32)), axis=1)
    sq_block = jnp.sum(jnp.square(block_rows.astype(jnp.float32)), axis=1)
    inner = lax.dot_general(
        examples, block_rows, (((1,), (1,)), ((), ())), preferred_element_type=jnp.float32
    )
    kernel = jnp.exp(
        -width_factor * (sq_rows[:, None] + sq_block[None, :] - 2.0 * inner) / features
    ).astype(jnp.bfloat16)
    residual_low = residuals.astype(jnp.bfloat16)
    grad_part = lax.dot_general(
        kernel, residual_low, (((0,), (0,)), ((), ())), preferred_element_type=jnp.float32
    )
    gram_part = lax.dot_general(
        kernel, kernel, (((0,), (0,)), ((), ())), preferred_element_type=jnp.float32
    )
    own_coef = lax.dynamic_slice_in_dim(coefficients, offset, BLOCK, 0)
    weight_own = jnp.where(is_owner, total_examples * ridge, 0.0).astype(jnp.float32)
    grad_part = grad_part - weight_own * own_coef
    packed = [gram_part[:c // 256 * 256 + 256, c:c + NB] for c in range(0, BLOCK, NB)]
    packed += [grad_part[:, c:c + NB] for c in range(0, grad_part.shape[1], NB)]
    sums = all_sum(jnp.concatenate(packed, axis=0), SUM_PARTS, 2, "sum_spread")
    update, update_low = solve(sums, BLOCK, grad_part.shape[1], total_examples, ridge)
    new_residuals = residuals - jnp.dot(kernel, update_low, preferred_element_type=jnp.float32)
    updated = lax.dynamic_update_slice_in_dim(coefficients, own_coef + update, offset, 0)
    new_coefficients = jnp.where(is_owner, updated, coefficients)
    return (new_residuals, new_coefficients)


def solution(mesh):
    in_specs = (P(("row", "col"), None), P(("row", "col"), None), P(("row", "col"), None), P())
    out_specs = (P(("row", "col"), None), P(("row", "col"), None))
    return jax.shard_map(body, mesh=mesh, in_specs=in_specs, out_specs=out_specs, check_vma=False)
```

```python
import functools
import jax
import jax.numpy as jnp
from jax import lax
from jax.experimental import pallas as pl
from jax.experimental.pallas import tpu as pltpu
from jax.sharding import PartitionSpec as P

BLOCK = 1024

ridge = 0.001
width_factor = 0.5


BLOCK_PARTS = ((0, 512, 0, 384), (0, 512, 384, 384), (0, 512, 768, 256))
SUM_PARTS = ((0, 1152, 0, 128), (1152, 1152, 0, 128), (2304, 1280, 0, 128))
AXES = ("x", "y", "z")

def place():
    row, col = lax.axis_index("row"), lax.axis_index("col")
    return {"x": (col // 2) % 2 * 2 + row // 4, "y": col // 4, "z": row % 4, "core": col % 2}

def device(at):
    return (at["x"] % 2 * 4 + at["z"], at["y"] * 4 + at["x"] // 2 * 2 + at["core"])

def shifted(at, axis, by):
    size = 2 if axis == "core" else 4
    return device({**at, axis: (at[axis] + by) % size})

def sum_kernel(parts, unit, x_ref, out_ref, theirs, acc, slot1, slot2, slot3, core_sems, ring_sems):
    at = place()
    half = x_ref.shape[0] // 2
    barrier = pltpu.get_barrier_semaphore()
    peers = [("core", 1)] + [(a, o) for a in AXES for o in (1, 2, 3)]
    for axis, by in peers:
        pl.semaphore_signal(barrier, inc=1, device_id=shifted(at, axis, by), device_id_type=pl.DeviceIdType.MESH)
    pl.semaphore_wait(barrier, len(peers))
    sent = []

    def send(src, dst, sems, who):
        copy = pltpu.make_async_remote_copy(src_ref=src, dst_ref=dst, send_sem=sems.at[0], recv_sem=sems.at[1],
                                            device_id=who, device_id_type=pl.DeviceIdType.MESH)
        copy.start()
        sent.append(copy)
        return copy

    mine, other = at["core"] * half, (1 - at["core"]) * half
    orders = [tuple(AXES[(p + i) % 3] for i in range(3)) for p in range(len(parts))]

    def rows(start, n, c0, cn):
        return (pl.ds(pl.multiple_of(start, unit), n), pl.ds(c0, cn))

    def core_send(p, source, base, target, tbase, k):
        r, n, c0, cn = parts[p]
        return send(source.at[rows(base + r, n, c0, cn)], target.at[rows(tbase + r, n, c0, cn)],
                    core_sems.at[k, p], shifted(at, "core", 1))

    P = range(len(parts))
    pending = [core_send(p, x_ref, other, theirs, 0, 0) for p in P]
    nxt = []
    for p in P:
        r, n, c0, cn = parts[p]
        pending[p].wait_recv()
        acc[rows(r, n, c0, cn)] = x_ref[rows(mine + r, n, c0, cn)] + theirs[rows(r, n, c0, cn)]
        q = n // 4
        a = orders[p][0]
        nxt.append([send(acc.at[rows(r + (at[a] + o) % 4 * q, q, c0, cn)], slot1.at[o - 1, pl.ds(r // 4, q), pl.ds(c0, cn)],
                         ring_sems.at[0, p, o - 1], shifted(at, a, o)) for o in (1, 2, 3)])
    pending, nxt = nxt, []
    begin = []
    for p in P:
        r, n, c0, cn = parts[p]
        for c in pending[p]:
            c.wait_recv()
        q, s = n // 4, n // 16
        a, b = orders[p][:2]
        start = r + at[a] * q
        begin.append(start)
        sl = lambda o: slot1[o - 1, pl.ds(r // 4, q), pl.ds(c0, cn)]
        acc[rows(start, q, c0, cn)] = (acc[rows(start, q, c0, cn)] + sl(2)) + (sl(1) + sl(3))
        nxt.append([send(acc.at[rows(start + (at[b] + o) % 4 * s, s, c0, cn)], slot2.at[o - 1, pl.ds(r // 16, s), pl.ds(c0, cn)],
                         ring_sems.at[1, p, o - 1], shifted(at, b, o)) for o in (1, 2, 3)])
    pending, nxt = nxt, []
    fine = []
    for p in P:
        r, n, c0, cn = parts[p]
        for c in pending[p]:
            c.wait_recv()
        s = n // 16
        b, d = orders[p][1:]
        start = begin[p] + at[b] * s
        fine.append(start)
        sl = lambda o: slot2[o - 1, pl.ds(r // 16, s), pl.ds(c0, cn)]
        acc[rows(start, s, c0, cn)] = (acc[rows(start, s, c0, cn)] + sl(2)) + (sl(1) + sl(3))
        nxt.append([send(acc.at[rows(start, s, c0, cn)], slot3.at[o - 1, pl.ds(r // 16, s), pl.ds(c0, cn)],
                         ring_sems.at[2, p, o - 1], shifted(at, d, o)) for o in (1, 2, 3)])
    pending, nxt = nxt, []
    for p in P:
        r, n, c0, cn = parts[p]
        for c in pending[p]:
            c.wait_recv()
        s = n // 16
        b = orders[p][1]
        sl = lambda o: slot3[o - 1, pl.ds(r // 16, s), pl.ds(c0, cn)]
        out_ref[rows(mine + fine[p], s, c0, cn)] = (acc[rows(fine[p], s, c0, cn)] + sl(2)) + (sl(1) + sl(3))
        here = out_ref.at[rows(mine + fine[p], s, c0, cn)]
        nxt.append([send(here, here, ring_sems.at[3, p, o - 1], shifted(at, b, o)) for o in (1, 2, 3)])
    pending, nxt = nxt, []
    for p in P:
        r, n, c0, cn = parts[p]
        for c in pending[p]:
            c.wait_recv()
        q = n // 4
        a = orders[p][0]
        here = out_ref.at[rows(mine + begin[p], q, c0, cn)]
        nxt.append([send(here, here, ring_sems.at[4, p, o - 1], shifted(at, a, o)) for o in (1, 2, 3)])
    pending, nxt = nxt, []
    for p in P:
        for c in pending[p]:
            c.wait_recv()
        nxt.append(core_send(p, out_ref, mine, out_ref, mine, 1))
    for p in P:
        nxt[p].wait_recv()
    for copy in sent:
        copy.wait_send()

def all_sum(x, parts, collective_id, name):
    n, w = x.shape
    half = n // 2
    unit = 16 if x.dtype == jnp.bfloat16 else 8
    dt = x.dtype
    return pl.pallas_call(
        functools.partial(sum_kernel, parts, unit),
        out_shape=jax.ShapeDtypeStruct(x.shape, dt),
        in_specs=[pl.BlockSpec(memory_space=pltpu.VMEM)],
        out_specs=pl.BlockSpec(memory_space=pltpu.VMEM),
        scratch_shapes=[
            pltpu.VMEM((half, w), dt), pltpu.VMEM((half, w), dt),
            pltpu.VMEM((3, half // 4, w), dt), pltpu.VMEM((3, half // 16, w), dt), pltpu.VMEM((3, half // 16, w), dt),
            pltpu.SemaphoreType.DMA((2, 3, 2)), pltpu.SemaphoreType.DMA((5, 3, 3, 2)),
        ],
        compiler_params=pltpu.CompilerParams(collective_id=collective_id, has_side_effects=True, vmem_limit_bytes=18 * 2**20),
        name=name,
    )(x)


CHUNK = 256

def gram_kernel(examples_ref, block_ref, sq_ref, residuals_ref, kt_ref, sums_ref, sqb):
    n, features = block_ref.shape
    count = examples_ref.shape[0]
    blk = block_ref[...].astype(jnp.float32)
    sqb[...] = jnp.broadcast_to(jnp.sum(blk * blk, axis=1, keepdims=True), sqb.shape)

    @pl.loop(0, count // CHUNK)
    def _(i):
        at = pl.multiple_of(i * CHUNK, CHUNK)
        inner = lax.dot_general(block_ref[...], examples_ref[pl.ds(at, CHUNK), :], (((1,), (1,)), ((), ())),
                                preferred_element_type=jnp.float32)
        left = sqb[...]
        left = jnp.concatenate([left] * (CHUNK // 128), axis=1)
        distance = sq_ref[:, pl.ds(at, CHUNK)] + left - 2.0 * inner
        kt_ref[:, pl.ds(at, CHUNK)] = jnp.exp(distance * (-width_factor / features)).astype(jnp.bfloat16)

    at = 0
    for c in range(0, n, 256):
        part = lax.dot_general(kt_ref[:c + 256, :], kt_ref[c:c + 256, :], (((1,), (1,)), ((), ())),
                               preferred_element_type=jnp.float32)
        for h in range(0, 256, 128):
            sums_ref[at:at + c + 256, :] = part[:, h:h + 128]
            at += c + 256
    part = jnp.dot(kt_ref[...], residuals_ref[...].astype(jnp.bfloat16), preferred_element_type=jnp.float32)
    for h in range(0, part.shape[1], 128):
        sums_ref[at:at + n, :] = part[:, h:h + 128]
        at += n

def gram(examples, block_rows, sq_rows, residuals):
    n = block_rows.shape[0]
    count, outputs = residuals.shape
    packed = 2 * sum(range(256, n + 1, 256)) + n * outputs // 128
    return pl.pallas_call(
        gram_kernel,
        out_shape=(jax.ShapeDtypeStruct((n, count), jnp.bfloat16), jax.ShapeDtypeStruct((packed, 128), jnp.float32)),
        in_specs=[pl.BlockSpec(memory_space=pltpu.VMEM)] * 4,
        out_specs=[pl.BlockSpec(memory_space=pltpu.VMEM)] * 2,
        scratch_shapes=[pltpu.VMEM((n, 128), jnp.float32)],
        compiler_params=pltpu.CompilerParams(vmem_limit_bytes=32 * 2**20),
        name="kernel_and_gram",
    )(examples, block_rows, sq_rows, residuals)


HI = lax.Precision.HIGHEST
NB = 128

def dot(a, b, ca, cb):
    return lax.dot_general(a, b, (((ca,), (cb,)), ((), ())), precision=HI, preferred_element_type=jnp.float32)

def split3(v):
    h = v.astype(jnp.bfloat16).astype(jnp.float32)
    r = v - h
    m = r.astype(jnp.bfloat16).astype(jnp.float32)
    return h, m, r - m

def factor(M):
    sub = lax.broadcasted_iota(jnp.int32, (8, 128), 0)
    sub2 = lax.broadcasted_iota(jnp.int32, (8, 256), 0)
    lane = lax.broadcasted_iota(jnp.int32, (8, 128), 1)
    for q in range(16):
        r0 = 8 * q
        look = q < 15
        top = M[r0:r0 + 8, :]
        ct = [jnp.broadcast_to(top[:, r0 + j:r0 + j + 1], (8, 128)) for j in range(8)]
        if look:
            bot = M[r0 + 8:r0 + 16, :]
            cb = [jnp.broadcast_to(bot[:, r0 + j:r0 + j + 1], (8, 128)) for j in range(8)]
        for j in range(8):
            r = lax.rsqrt(ct[j][j:j + 1, :])
            r2 = jnp.concatenate([r, r], axis=1)
            row = top[j:j + 1, :] * r2
            mt = jnp.where(sub > j, ct[j] * r, 0.0)
            mt2 = jnp.concatenate([mt, mt], axis=1)
            rows_k = {k: ct[k][j:j + 1, :] * r for k in range(j + 1, 8)}
            top = jnp.where(sub2 == j, row, top - mt2 * row)
            for k in range(j + 1, 8):
                ct[k] = ct[k] - mt * rows_k[k]
            if look:
                mb = cb[j] * r
                mb2 = jnp.concatenate([mb, mb], axis=1)
                bot = bot - mb2 * row
                for k in range(j + 1, 8):
                    cb[k] = cb[k] - mb * rows_k[k]
        M[r0:r0 + 8, :] = top
        if look:
            M[r0 + 8:r0 + 16, :] = bot
        if q < 14:
            h, m, l = split3(top)
            keep = lane >= r0 + 16
            hl, ml, ll = [jnp.where(keep, v[:, :128], 0.0) for v in (h, m, l)]
            lhs = jnp.concatenate([hl, hl, ml, hl, ml, ll], axis=0).astype(jnp.bfloat16)
            rhs = jnp.concatenate([h, m, h, l, m, h], axis=0).astype(jnp.bfloat16)
            res = lax.dot_general(lhs, rhs, (((0,), (0,)), ((), ())), preferred_element_type=jnp.float32)
            M[r0 + 16:, :] = M[r0 + 16:, :] - res[r0 + 16:, :]

def solve_kernel(scale, ridge, sums_ref, upd_ref, low_ref, S, G, M, W):
    n = S.shape[0]
    nb = n // NB
    eye = (lax.broadcasted_iota(jnp.int32, (NB, NB), 0) == lax.broadcasted_iota(jnp.int32, (NB, NB), 1)).astype(jnp.float32)
    at = 0
    for c in range(0, n, NB):
        depth = c // 256 * 256 + 256
        S[0:depth, c:c + NB] = sums_ref[at:at + depth, :] * scale
        at += depth
    for c in range(0, G.shape[1], NB):
        G[:, c:c + NB] = sums_ref[at:at + n, :] * scale
        at += n
    for k in range(nb):
        a, b = k * NB, (k + 1) * NB
        M[:, :NB] = S[a:b, a:b] + ridge * eye
        M[:, NB:] = eye
        factor(M)
        w = M[:, NB:]
        W[a:b, :] = w
        G[a:b, :] = dot(w, G[a:b, :], 1, 0)
        if k < nb - 1:
            u = dot(w, S[a:b, b:], 1, 0)
            S[a:b, b:] = u
            for i in range(b, n, NB):
                S[i:i + NB, i:] = S[i:i + NB, i:] - dot(u[:, i - b:i - b + NB], u[:, i - b:], 0, 0)
            G[b:, :] = G[b:, :] - dot(u, G[a:b, :], 0, 0)
    for k in reversed(range(nb)):
        a, b = k * NB, (k + 1) * NB
        y = G[a:b, :]
        if k < nb - 1:
            y = y - dot(S[a:b, b:], G[b:, :], 1, 0)
        G[a:b, :] = dot(W[a:b, :], y, 0, 0)
    upd_ref[...] = G[...]
    low_ref[...] = G[...].astype(jnp.bfloat16)

def solve(sums, n, o, total, ridge):
    return pl.pallas_call(
        functools.partial(solve_kernel, 1.0 / total, ridge),
        out_shape=(jax.ShapeDtypeStruct((n, o), jnp.float32), jax.ShapeDtypeStruct((n, o), jnp.bfloat16)),
        in_specs=[pl.BlockSpec(memory_space=pltpu.VMEM)],
        out_specs=[pl.BlockSpec(memory_space=pltpu.VMEM)] * 2,
        scratch_shapes=[pltpu.VMEM((n, n), jnp.float32), pltpu.VMEM((n, o), jnp.float32), pltpu.VMEM((NB, 2 * NB), jnp.float32), pltpu.VMEM((n, NB), jnp.float32)],
        compiler_params=pltpu.CompilerParams(vmem_limit_bytes=24 * 2**20),
        name="solve_block",
    )(sums)


def body(examples, residuals, coefficients, block_index):
    rows_here = examples.shape[0]
    per_device = rows_here // BLOCK
    devices_all = lax.axis_size(("row", "col"))
    total_examples = rows_here * devices_all
    chosen = block_index[0]
    owner_rank = chosen // per_device
    offset = chosen % per_device * BLOCK
    my_rank = lax.axis_index(("row", "col"))
    is_owner = owner_rank == my_rank
    my_block = lax.dynamic_slice_in_dim(examples, offset, BLOCK, 0)
    kept = jnp.where(is_owner, my_block, 0).astype(my_block.dtype)
    block_rows = all_sum(kept, BLOCK_PARTS, 1, "block_spread")
    sq_rows = jnp.sum(jnp.square(examples.astype(jnp.float32)), axis=1)[None, :]
    kernel_t, packed = gram(examples, block_rows, sq_rows, residuals)
    own_coef = lax.dynamic_slice_in_dim(coefficients, offset, BLOCK, 0)
    weight_own = jnp.where(is_owner, total_examples * ridge, 0.0).astype(jnp.float32)
    halves = [own_coef[:, c:c + NB] for c in range(0, own_coef.shape[1], NB)]
    first = packed.shape[0] - len(halves) * BLOCK
    packed = packed.at[first:].add(-weight_own * jnp.concatenate(halves, axis=0))
    sums = all_sum(packed, SUM_PARTS, 2, "sum_spread")
    update, update_low = solve(sums, BLOCK, own_coef.shape[1], total_examples, ridge)
    change = lax.dot_general(kernel_t, update_low, (((0,), (0,)), ((), ())), preferred_element_type=jnp.float32)
    new_residuals = residuals - change
    updated = lax.dynamic_update_slice_in_dim(coefficients, own_coef + update, offset, 0)
    new_coefficients = jnp.where(is_owner, updated, coefficients)
    return (new_residuals, new_coefficients)


def solution(mesh):
    in_specs = (P(("row", "col"), None), P(("row", "col"), None), P(("row", "col"), None), P())
    out_specs = (P(("row", "col"), None), P(("row", "col"), None))
    return jax.shard_map(body, mesh=mesh, in_specs=in_specs, out_specs=out_specs, check_vma=False)
```

```python
import functools
import jax
import jax.numpy as jnp
from jax import lax
from jax.experimental import pallas as pl
from jax.experimental.pallas import tpu as pltpu
from jax.sharding import PartitionSpec as P

BLOCK = 1024

ridge = 0.001
width_factor = 0.5


BLOCK_PARTS = tuple((r, 256, c, n) for r in (0, 256) for c, n in ((0, 384), (384, 384), (768, 256)))
SUM_PARTS = tuple((r, n, 0, 128) for r, n in ((0, 640), (640, 640), (1280, 512), (1792, 640), (2432, 640), (3072, 512)))
AXES = ("x", "y", "z")
NB = 128
CHUNK = 256
WIDE = 512
HALF = 3584
GRAM_AT = (HALF + 3072, HALF + 3328, HALF + 2560, 3072, HALF + 1024, HALF + 1792, 0, HALF)
GRAD_AT = (1024, 2048)

def depth_of(j):
    return (j // 2 + 1) * 256

def place():
    row, col = lax.axis_index("row"), lax.axis_index("col")
    return {"x": (col // 2) % 2 * 2 + row // 4, "y": col // 4, "z": row % 4, "core": col % 2}

def device(at):
    return (at["x"] % 2 * 4 + at["z"], at["y"] * 4 + at["x"] // 2 * 2 + at["core"])

def shifted(at, axis, by):
    size = 2 if axis == "core" else 4
    return device({**at, axis: (at[axis] + by) % size})

class Sum:
    def __init__(self, at, parts, unit, x, out, theirs, acc, slot1, slot2, slot3, core_sems, ring_sems, sent):
        self.__dict__.update(locals())
        half = x.shape[0] // 2
        self.mine, self.other = at["core"] * half, (1 - at["core"]) * half
        self.orders = [tuple(AXES[(p + i) % 3] for i in range(3)) for p in range(len(parts))]
        self.wait, self.begin, self.fine = {}, {}, {}

    def rows(self, start, n, c0, cn):
        return (pl.ds(pl.multiple_of(start, self.unit), n), pl.ds(c0, cn))

    def send(self, src, dst, sems, who):
        copy = pltpu.make_async_remote_copy(src_ref=src, dst_ref=dst, send_sem=sems.at[0], recv_sem=sems.at[1],
                                            device_id=who, device_id_type=pl.DeviceIdType.MESH)
        copy.start()
        self.sent.append(copy)
        return copy

    def arrived(self, p):
        for copy in self.wait[p]:
            copy.wait_recv()
        return self.parts[p]

    def to_peers(self, p, axis, stage, piece):
        self.wait[p] = [self.send(*piece(o), self.ring_sems.at[stage, p, o - 1], shifted(self.at, axis, o)) for o in (1, 2, 3)]

    def total(self, own, slot, where):
        sl = lambda o: slot[(o - 1,) + where]
        return (self.acc[own] + sl(2)) + (sl(1) + sl(3))

    def pair(self, p):
        r, n, c0, cn = self.parts[p]
        self.wait[p] = [self.send(self.x.at[self.rows(self.other + r, n, c0, cn)], self.theirs.at[self.rows(r, n, c0, cn)],
                                  self.core_sems.at[0, p], shifted(self.at, "core", 1))]

    def scatter1(self, p):
        r, n, c0, cn = self.arrived(p)
        self.acc[self.rows(r, n, c0, cn)] = self.x[self.rows(self.mine + r, n, c0, cn)] + self.theirs[self.rows(r, n, c0, cn)]
        q, a = n // 4, self.orders[p][0]
        self.to_peers(p, a, 0, lambda o: (self.acc.at[self.rows(r + (self.at[a] + o) % 4 * q, q, c0, cn)],
                                          self.slot1.at[o - 1, pl.ds(r // 4, q), pl.ds(c0, cn)]))

    def scatter2(self, p):
        r, n, c0, cn = self.arrived(p)
        q, s = n // 4, n // 16
        a, b = self.orders[p][:2]
        start = self.begin[p] = r + self.at[a] * q
        own = self.rows(start, q, c0, cn)
        self.acc[own] = self.total(own, self.slot1, (pl.ds(r // 4, q), pl.ds(c0, cn)))
        self.to_peers(p, b, 1, lambda o: (self.acc.at[self.rows(start + (self.at[b] + o) % 4 * s, s, c0, cn)],
                                          self.slot2.at[o - 1, pl.ds(r // 16, s), pl.ds(c0, cn)]))

    def exchange(self, p):
        r, n, c0, cn = self.arrived(p)
        s = n // 16
        b, d = self.orders[p][1:]
        start = self.fine[p] = self.begin[p] + self.at[b] * s
        own = self.rows(start, s, c0, cn)
        self.acc[own] = self.total(own, self.slot2, (pl.ds(r // 16, s), pl.ds(c0, cn)))
        self.to_peers(p, d, 2, lambda o: (self.acc.at[own], self.slot3.at[o - 1, pl.ds(r // 16, s), pl.ds(c0, cn)]))

    def gather2(self, p):
        r, n, c0, cn = self.arrived(p)
        s = n // 16
        here = self.rows(self.mine + self.fine[p], s, c0, cn)
        self.out[here] = self.total(self.rows(self.fine[p], s, c0, cn), self.slot3, (pl.ds(r // 16, s), pl.ds(c0, cn)))
        self.to_peers(p, self.orders[p][1], 3, lambda o: (self.out.at[here],) * 2)

    def gather1(self, p):
        r, n, c0, cn = self.arrived(p)
        here = self.rows(self.mine + self.begin[p], n // 4, c0, cn)
        self.to_peers(p, self.orders[p][0], 4, lambda o: (self.out.at[here],) * 2)

    def pair_back(self, p):
        r, n, c0, cn = self.arrived(p)
        here = self.out.at[self.rows(self.mine + r, n, c0, cn)]
        self.wait[p] = [self.send(here, here, self.core_sems.at[1, p], shifted(self.at, "core", 1))]

STEPS = ("scatter1", "scatter2", "exchange", "gather2", "gather1", "pair_back")

def step_kernel(x_ref, examples_ref, residuals_ref, shift_ref, kt_ref, sums_ref,
                block, theirs_b, acc_b, slot1_b, slot2_b, slot3_b, core_b, ring_b,
                parts, theirs_s, acc_s, slot1_s, slot2_s, slot3_s, core_s, ring_s,
                ex, res, sqb, sqe, load_sems):
    at = place()
    n, features = block.shape
    count = ex.shape[0]
    barrier = pltpu.get_barrier_semaphore()
    peers = [("core", 1)] + [(a, o) for a in AXES for o in (1, 2, 3)]
    for axis, by in peers:
        pl.semaphore_signal(barrier, inc=1, device_id=shifted(at, axis, by), device_id_type=pl.DeviceIdType.MESH)
    loads = [pltpu.make_async_copy(examples_ref, ex, load_sems.at[0]), pltpu.make_async_copy(residuals_ref, res, load_sems.at[1])]
    for load in loads:
        load.start()
    pl.semaphore_wait(barrier, len(peers))
    sent = []
    spread = Sum(at, BLOCK_PARTS, 16, x_ref, block, theirs_b, acc_b, slot1_b, slot2_b, slot3_b, core_b, ring_b, sent)
    add = Sum(at, SUM_PARTS, 8, parts, sums_ref, theirs_s, acc_s, slot1_s, slot2_s, slot3_s, core_s, ring_s, sent)
    P = range(6)
    for p in P:
        spread.pair(p)
    for p in P:
        spread.scatter1(p)
    loads[0].wait()

    def squares(first, last):
        @pl.loop(first, last)
        def _(i):
            here = pl.ds(pl.multiple_of(i * CHUNK, CHUNK), CHUNK)
            total = jnp.zeros((CHUNK, 128), jnp.float32)
            for f in range(0, features, 128):
                e = ex[here, f:f + 128].astype(jnp.float32)
                total = total + e * e
            high = total.astype(jnp.bfloat16)
            rest = total - high.astype(jnp.float32)
            middle = rest.astype(jnp.bfloat16)
            low = (rest - middle.astype(jnp.float32)).astype(jnp.bfloat16)
            sqe[:, here] = lax.dot_general(jnp.full((16, 384), 1.0, jnp.bfloat16), jnp.concatenate([high, middle, low], axis=1),
                                           (((1,), (1,)), ((), ())), preferred_element_type=jnp.float32)[:8, :] * (-width_factor / features)

    steps = count // CHUNK
    squares(0, steps // 2)
    for name in STEPS[1:-1]:
        for p in P:
            getattr(spread, name)(p)
        if name == "scatter2":
            squares(steps // 2, steps)
            loads[1].wait()

    def form(start, rows):
        mine = pl.ds(pl.multiple_of(start, rows), rows)
        b = block[mine, :].astype(jnp.float32)
        sqb[mine, :] = jnp.broadcast_to(jnp.sum(b * b, axis=1, keepdims=True) * (-width_factor / features), (rows, 128))

        @pl.loop(0, count // WIDE, unroll=2)
        def _(i):
            here = pl.ds(pl.multiple_of(i * WIDE, WIDE), WIDE)
            inner = lax.dot_general(block[mine, :], ex[here, :], (((1,), (1,)), ((), ())), preferred_element_type=jnp.float32)
            left = jnp.concatenate([sqb[mine, :]] * (WIDE // 128), axis=1)
            kt_ref[mine, here] = jnp.exp(sqe[0:1, here] + left + inner * (2.0 * width_factor / features)).astype(jnp.bfloat16)

    for wave in (0, 1):
        for p in range(3 * wave, 3 * wave + 3):
            spread.pair_back(p)
        form(spread.mine + wave * (n // 4), n // 4)
    for p in P:
        spread.arrived(p)
    form(spread.other, n // 2)

    def upper(c):
        part = lax.dot_general(kt_ref[:c + 256, :], kt_ref[c:c + 256, :], (((1,), (1,)), ((), ())), preferred_element_type=jnp.float32)
        for j in (c // 128, c // 128 + 1):
            to = GRAM_AT[j]
            parts[to:to + c + 256, :] = part[:, j * 128 - c:j * 128 - c + 128]

    upper(768)
    add.pair(0)
    upper(512)
    part = jnp.dot(kt_ref[...], res[...].astype(jnp.bfloat16), preferred_element_type=jnp.float32) - shift_ref[...]
    for h, to in enumerate(GRAD_AT):
        parts[to:to + n, :] = part[:, h * 128:h * 128 + 128]
    for p in (1, 2, 3):
        add.pair(p)
    upper(256)
    add.pair(4)
    upper(0)
    add.pair(5)
    for p in P:
        add.scatter1(p)
    for name in STEPS[1:]:
        for p in P:
            getattr(add, name)(p)
    for p in P:
        add.arrived(p)
    for copy in sent:
        copy.wait_send()

def sum_scratch(rows, columns, dt):
    half = rows // 2
    return [pltpu.VMEM((half, columns), dt), pltpu.VMEM((half, columns), dt),
            pltpu.VMEM((3, half // 4, columns), dt), pltpu.VMEM((3, half // 16, columns), dt), pltpu.VMEM((3, half // 16, columns), dt),
            pltpu.SemaphoreType.DMA((2, 6, 2)), pltpu.SemaphoreType.DMA((5, 6, 3, 2))]

def sums_and_kernel(kept, examples, residuals, shift):
    n, features = kept.shape
    count, outputs = residuals.shape
    f32, bf16 = jnp.float32, jnp.bfloat16
    vmem, any_ = pl.BlockSpec(memory_space=pltpu.VMEM), pl.BlockSpec(memory_space=pl.ANY)
    return pl.pallas_call(
        step_kernel,
        out_shape=(jax.ShapeDtypeStruct((n, count), bf16), jax.ShapeDtypeStruct((2 * HALF, 128), f32)),
        in_specs=[vmem, any_, any_, vmem],
        out_specs=[vmem, vmem],
        scratch_shapes=[pltpu.VMEM((n, features), bf16)] + sum_scratch(n, features, bf16)
        + [pltpu.VMEM((2 * HALF, 128), f32)] + sum_scratch(2 * HALF, 128, f32)
        + [pltpu.VMEM((count, features), bf16), pltpu.VMEM((count, outputs), f32), pltpu.VMEM((n, 128), f32), pltpu.VMEM((8, count), f32),
           pltpu.SemaphoreType.DMA((2,))],
        compiler_params=pltpu.CompilerParams(collective_id=1, has_side_effects=True, vmem_limit_bytes=42 * 2**20),
        name="spread_and_sum",
    )(kept, examples, residuals, shift)


def split3(v):
    h = v.astype(jnp.bfloat16).astype(jnp.float32)
    r = v - h
    m = r.astype(jnp.bfloat16).astype(jnp.float32)
    return h, m, r - m

def stacks(v, axis):
    h, m, l = [x.astype(jnp.bfloat16) for x in split3(v)]
    return jnp.concatenate([h, h, m, h, m, l], axis=axis), jnp.concatenate([h, m, h, l, m, h], axis=axis)

def left(v, axis):
    return stacks(v, axis)[0]

def right(v, axis):
    return stacks(v, axis)[1]

def dot(a, b, ca, cb):
    return lax.dot_general(a, b, (((ca,), (cb,)), ((), ())), preferred_element_type=jnp.float32)

def factor(M, tasks=()):
    done = 0
    sub = lax.broadcasted_iota(jnp.int32, (8, 128), 0)
    sub2 = lax.broadcasted_iota(jnp.int32, (8, 256), 0)
    lane = lax.broadcasted_iota(jnp.int32, (8, 128), 1)
    for q in range(16):
        r0 = 8 * q
        look = q < 15
        top = M[r0:r0 + 8, :]
        ct = [jnp.broadcast_to(top[:, r0 + j:r0 + j + 1], (8, 128)) for j in range(8)]
        if look:
            bot = M[r0 + 8:r0 + 16, :]
            cb = [jnp.broadcast_to(bot[:, r0 + j:r0 + j + 1], (8, 128)) for j in range(8)]
        for j in range(8):
            r = lax.rsqrt(ct[j][j:j + 1, :])
            r2 = jnp.concatenate([r, r], axis=1)
            row = top[j:j + 1, :] * r2
            mt = jnp.where(sub > j, ct[j] * r, 0.0)
            mt2 = jnp.concatenate([mt, mt], axis=1)
            rows_k = {k: ct[k][j:j + 1, :] * r for k in range(j + 1, 8)}
            top = jnp.where(sub2 == j, row, top - mt2 * row)
            for k in range(j + 1, 8):
                ct[k] = ct[k] - mt * rows_k[k]
            if look:
                mb = cb[j] * r
                mb2 = jnp.concatenate([mb, mb], axis=1)
                bot = bot - mb2 * row
                for k in range(j + 1, 8):
                    cb[k] = cb[k] - mb * rows_k[k]
        M[r0:r0 + 8, :] = top
        if look:
            M[r0 + 8:r0 + 16, :] = bot
        if q < 14:
            h, m, l = split3(top)
            keep = lane >= r0 + 16
            hl, ml, ll = [jnp.where(keep, v[:, :128], 0.0) for v in (h, m, l)]
            lhs = jnp.concatenate([hl, hl, ml, hl, ml, ll], axis=0).astype(jnp.bfloat16)
            rhs = jnp.concatenate([h, m, h, l, m, h], axis=0).astype(jnp.bfloat16)
            res = lax.dot_general(lhs, rhs, (((0,), (0,)), ((), ())), preferred_element_type=jnp.float32)
            M[r0 + 16:, :] = M[r0 + 16:, :] - res[r0 + 16:, :]
        until = len(tasks) * (q + 1) // 14 if q < 13 else len(tasks)
        for task in tasks[done:until]:
            task()
        done = max(done, until)

def solve_kernel(scale, ridge, sums_ref, upd_ref, low_ref, S, G, M, V, UL, UR):
    n = S.shape[0]
    nb = n // NB
    eye = (lax.broadcasted_iota(jnp.int32, (NB, NB), 0) == lax.broadcasted_iota(jnp.int32, (NB, NB), 1)).astype(jnp.float32)
    for j, to in enumerate(GRAM_AT):
        S[0:depth_of(j), j * NB:j * NB + NB] = sums_ref[to:to + depth_of(j), :] * scale
    for j, to in enumerate(GRAD_AT):
        G[:, j * NB:j * NB + NB] = sums_ref[to:to + n, :] * scale

    def after(k, w):
        a, b = k * NB, (k + 1) * NB
        wl = left(w, 1)
        made = {}

        def keep(lo, hi):
            u = dot(wl, right(S[a:b, lo:hi], 0), 1, 0)
            S[a:b, lo:hi] = u
            UL[:, lo:hi], UR[:, lo:hi] = stacks(u, 0)

        def row(i, lo, hi):
            S[i:i + NB, lo:hi] = S[i:i + NB, lo:hi] - dot(UL[:, i:i + NB], UR[:, lo:hi], 0, 0)

        def forward():
            y = dot(wl, right(G[a:b, :], 0), 1, 0)
            G[a:b, :] = y
            made["y"] = right(y, 0)
            made["w"] = left(w, 0)

        def lower(i):
            G[i:i + NB, :] = G[i:i + NB, :] - dot(UL[:, i:i + NB], made["y"], 0, 0)

        def back():
            G[a:b, :] = dot(made["w"], made["y"], 0, 0)
            if b < n:
                V[a:b, b:] = dot(made["w"], UR[:, b:], 0, 0)

        tasks = []
        if b < n:
            c = b + NB
            keep(b, c)
            row(b, b, c)
            if c < n:
                tasks.append(lambda: keep(c, n))
                tasks.append(lambda: row(b, c, n))
        tasks.append(forward)
        for i in range(b, n, NB):
            if i > b:
                tasks.append(functools.partial(row, i, i, n))
            tasks.append(functools.partial(lower, i))
        tasks.append(back)
        return tasks

    tasks = []
    for k in range(nb):
        a, b = k * NB, (k + 1) * NB
        M[:, :NB] = S[a:b, a:b] + ridge * eye
        M[:, NB:] = eye
        factor(M, tasks)
        tasks = after(k, M[:, NB:])
    for task in tasks:
        task()
    for j in range(n - NB, 0, -NB):
        x = right(G[j:j + NB, :], 0)
        for i in range(j - NB, -1, -NB):
            G[i:i + NB, :] = G[i:i + NB, :] - dot(left(V[i:i + NB, j:j + NB], 1), x, 1, 0)
    upd_ref[...] = G[...]
    low_ref[...] = G[...].astype(jnp.bfloat16)

def solve(sums, n, o, total, ridge):
    return pl.pallas_call(
        functools.partial(solve_kernel, 1.0 / total, ridge),
        out_shape=(jax.ShapeDtypeStruct((n, o), jnp.float32), jax.ShapeDtypeStruct((n, o), jnp.bfloat16)),
        in_specs=[pl.BlockSpec(memory_space=pltpu.VMEM)],
        out_specs=[pl.BlockSpec(memory_space=pltpu.VMEM)] * 2,
        scratch_shapes=[pltpu.VMEM((n, n), jnp.float32), pltpu.VMEM((n, o), jnp.float32), pltpu.VMEM((NB, 2 * NB), jnp.float32), pltpu.VMEM((n, n), jnp.float32), pltpu.VMEM((6 * NB, n), jnp.bfloat16), pltpu.VMEM((6 * NB, n), jnp.bfloat16)],
        compiler_params=pltpu.CompilerParams(vmem_limit_bytes=32 * 2**20),
        name="solve_block",
    )(sums)


def body(examples, residuals, coefficients, block_index):
    rows_here = examples.shape[0]
    per_device = rows_here // BLOCK
    devices_all = lax.axis_size(("row", "col"))
    total_examples = rows_here * devices_all
    chosen = block_index[0]
    owner_rank = chosen // per_device
    offset = chosen % per_device * BLOCK
    my_rank = lax.axis_index(("row", "col"))
    is_owner = owner_rank == my_rank
    my_block = lax.dynamic_slice_in_dim(examples, offset, BLOCK, 0)
    kept = jnp.where(is_owner, my_block, 0).astype(my_block.dtype)
    own_coef = lax.dynamic_slice_in_dim(coefficients, offset, BLOCK, 0)
    weight_own = jnp.where(is_owner, total_examples * ridge, 0.0).astype(jnp.float32)
    kernel_t, sums = sums_and_kernel(kept, examples, residuals, weight_own * own_coef)
    update, update_low = solve(sums, BLOCK, own_coef.shape[1], total_examples, ridge)
    change = lax.dot_general(kernel_t, update_low, (((0,), (0,)), ((), ())), preferred_element_type=jnp.float32)
    new_residuals = residuals - change
    updated = lax.dynamic_update_slice_in_dim(coefficients, own_coef + update, offset, 0)
    new_coefficients = jnp.where(is_owner, updated, coefficients)
    return (new_residuals, new_coefficients)


def solution(mesh):
    in_specs = (P(("row", "col"), None), P(("row", "col"), None), P(("row", "col"), None), P())
    out_specs = (P(("row", "col"), None), P(("row", "col"), None))
    return jax.shard_map(body, mesh=mesh, in_specs=in_specs, out_specs=out_specs, check_vma=False)
```

```python
import functools
import jax
import jax.numpy as jnp
from jax import lax
from jax.experimental import pallas as pl
from jax.experimental.pallas import tpu as pltpu
from jax.sharding import PartitionSpec as P

BLOCK = 1024

ridge = 0.001
width_factor = 0.5


BLOCK_PARTS = tuple((r, 256, c, n) for r in (0, 256) for c, n in ((0, 384), (384, 384), (768, 256)))
SUM_PARTS = tuple((r, n, 0, 128) for r, n in ((0, 640), (640, 640), (1280, 512), (1792, 640), (2432, 640), (3072, 512)))
AXES = ("x", "y", "z")
NB = 128
CHUNK = 256
WIDE = 512
HALF = 3584
GRAM_AT = (HALF + 3072, HALF + 3328, HALF + 2560, 3072, HALF + 1024, HALF + 1792, 0, HALF)
GRAD_AT = (1024, 2048)

def depth_of(j):
    return (j // 2 + 1) * 256

def place():
    row, col = lax.axis_index("row"), lax.axis_index("col")
    return {"x": (col // 2) % 2 * 2 + row // 4, "y": col // 4, "z": row % 4, "core": col % 2}

def device(at):
    return (at["x"] % 2 * 4 + at["z"], at["y"] * 4 + at["x"] // 2 * 2 + at["core"])

def shifted(at, axis, by):
    size = 2 if axis == "core" else 4
    return device({**at, axis: (at[axis] + by) % size})

class Sum:
    def __init__(self, at, parts, unit, x, out, theirs, acc, slot1, slot2, slot3, core_sems, ring_sems, sent):
        self.__dict__.update(locals())
        half = x.shape[0] // 2
        self.mine, self.other = at["core"] * half, (1 - at["core"]) * half
        self.orders = [tuple(AXES[(p + i) % 3] for i in range(3)) for p in range(len(parts))]
        self.wait, self.begin, self.fine = {}, {}, {}

    def rows(self, start, n, c0, cn):
        return (pl.ds(pl.multiple_of(start, self.unit), n), pl.ds(c0, cn))

    def send(self, src, dst, sems, who):
        copy = pltpu.make_async_remote_copy(src_ref=src, dst_ref=dst, send_sem=sems.at[0], recv_sem=sems.at[1],
                                            device_id=who, device_id_type=pl.DeviceIdType.MESH)
        copy.start()
        self.sent.append(copy)
        return copy

    def arrived(self, p):
        for copy in self.wait[p]:
            copy.wait_recv()
        return self.parts[p]

    def to_peers(self, p, axis, stage, piece):
        self.wait[p] = [self.send(*piece(o), self.ring_sems.at[stage, p, o - 1], shifted(self.at, axis, o)) for o in (1, 2, 3)]

    def total(self, own, slot, where):
        sl = lambda o: slot[(o - 1,) + where]
        return (self.acc[own] + sl(2)) + (sl(1) + sl(3))

    def pair(self, p):
        r, n, c0, cn = self.parts[p]
        self.wait[p] = [self.send(self.x.at[self.rows(self.other + r, n, c0, cn)], self.theirs.at[self.rows(r, n, c0, cn)],
                                  self.core_sems.at[0, p], shifted(self.at, "core", 1))]

    def scatter1(self, p):
        r, n, c0, cn = self.arrived(p)
        self.acc[self.rows(r, n, c0, cn)] = self.x[self.rows(self.mine + r, n, c0, cn)] + self.theirs[self.rows(r, n, c0, cn)]
        q, a = n // 4, self.orders[p][0]
        self.to_peers(p, a, 0, lambda o: (self.acc.at[self.rows(r + (self.at[a] + o) % 4 * q, q, c0, cn)],
                                          self.slot1.at[o - 1, pl.ds(r // 4, q), pl.ds(c0, cn)]))

    def scatter2(self, p):
        r, n, c0, cn = self.arrived(p)
        q, s = n // 4, n // 16
        a, b = self.orders[p][:2]
        start = self.begin[p] = r + self.at[a] * q
        own = self.rows(start, q, c0, cn)
        self.acc[own] = self.total(own, self.slot1, (pl.ds(r // 4, q), pl.ds(c0, cn)))
        self.to_peers(p, b, 1, lambda o: (self.acc.at[self.rows(start + (self.at[b] + o) % 4 * s, s, c0, cn)],
                                          self.slot2.at[o - 1, pl.ds(r // 16, s), pl.ds(c0, cn)]))

    def exchange(self, p):
        r, n, c0, cn = self.arrived(p)
        s = n // 16
        b, d = self.orders[p][1:]
        start = self.fine[p] = self.begin[p] + self.at[b] * s
        own = self.rows(start, s, c0, cn)
        self.acc[own] = self.total(own, self.slot2, (pl.ds(r // 16, s), pl.ds(c0, cn)))
        self.to_peers(p, d, 2, lambda o: (self.acc.at[own], self.slot3.at[o - 1, pl.ds(r // 16, s), pl.ds(c0, cn)]))

    def gather2(self, p):
        r, n, c0, cn = self.arrived(p)
        s = n // 16
        here = self.rows(self.mine + self.fine[p], s, c0, cn)
        self.out[here] = self.total(self.rows(self.fine[p], s, c0, cn), self.slot3, (pl.ds(r // 16, s), pl.ds(c0, cn)))
        self.to_peers(p, self.orders[p][1], 3, lambda o: (self.out.at[here],) * 2)

    def gather1(self, p):
        r, n, c0, cn = self.arrived(p)
        here = self.rows(self.mine + self.begin[p], n // 4, c0, cn)
        self.to_peers(p, self.orders[p][0], 4, lambda o: (self.out.at[here],) * 2)

    def pair_back(self, p):
        r, n, c0, cn = self.arrived(p)
        here = self.out.at[self.rows(self.mine + r, n, c0, cn)]
        self.wait[p] = [self.send(here, here, self.core_sems.at[1, p], shifted(self.at, "core", 1))]

STEPS = ("scatter1", "scatter2", "exchange", "gather2", "gather1", "pair_back")

def step_kernel(x_ref, examples_ref, residuals_ref, shift_ref, kt_ref, sums_ref,
                block, theirs_b, acc_b, slot1_b, slot2_b, slot3_b, core_b, ring_b,
                parts, theirs_s, acc_s, slot1_s, slot2_s, slot3_s, core_s, ring_s,
                ex, res, sqb, sqe, load_sems):
    at = place()
    n, features = block.shape
    count = ex.shape[0]
    barrier = pltpu.get_barrier_semaphore()
    peers = [("core", 1)] + [(a, o) for a in AXES for o in (1, 2, 3)]
    for axis, by in peers:
        pl.semaphore_signal(barrier, inc=1, device_id=shifted(at, axis, by), device_id_type=pl.DeviceIdType.MESH)
    loads = [pltpu.make_async_copy(examples_ref, ex, load_sems.at[0]), pltpu.make_async_copy(residuals_ref, res, load_sems.at[1])]
    for load in loads:
        load.start()
    pl.semaphore_wait(barrier, len(peers))
    sent = []
    spread = Sum(at, BLOCK_PARTS, 16, x_ref, block, theirs_b, acc_b, slot1_b, slot2_b, slot3_b, core_b, ring_b, sent)
    add = Sum(at, SUM_PARTS, 8, parts, sums_ref, theirs_s, acc_s, slot1_s, slot2_s, slot3_s, core_s, ring_s, sent)
    P = range(6)
    for p in P:
        spread.pair(p)
    for p in P:
        spread.scatter1(p)
    loads[0].wait()

    def squares(first, last):
        @pl.loop(first, last)
        def _(i):
            here = pl.ds(pl.multiple_of(i * CHUNK, CHUNK), CHUNK)
            total = jnp.zeros((CHUNK, 128), jnp.float32)
            for f in range(0, features, 128):
                e = ex[here, f:f + 128].astype(jnp.float32)
                total = total + e * e
            high = total.astype(jnp.bfloat16)
            rest = total - high.astype(jnp.float32)
            middle = rest.astype(jnp.bfloat16)
            low = (rest - middle.astype(jnp.float32)).astype(jnp.bfloat16)
            sqe[:, here] = lax.dot_general(jnp.full((16, 384), 1.0, jnp.bfloat16), jnp.concatenate([high, middle, low], axis=1),
                                           (((1,), (1,)), ((), ())), preferred_element_type=jnp.float32)[:8, :] * (-width_factor / features)

    steps = count // CHUNK
    squares(0, steps // 2)
    for name in STEPS[1:-1]:
        for p in P:
            getattr(spread, name)(p)
        if name == "scatter2":
            squares(steps // 2, steps)
            loads[1].wait()

    def form(start, rows):
        mine = pl.ds(pl.multiple_of(start, rows), rows)
        b = block[mine, :].astype(jnp.float32)
        sqb[mine, :] = jnp.broadcast_to(jnp.sum(b * b, axis=1, keepdims=True) * (-width_factor / features), (rows, 128))

        @pl.loop(0, count // WIDE, unroll=2)
        def _(i):
            here = pl.ds(pl.multiple_of(i * WIDE, WIDE), WIDE)
            inner = lax.dot_general(block[mine, :], ex[here, :], (((1,), (1,)), ((), ())), preferred_element_type=jnp.float32)
            left = jnp.concatenate([sqb[mine, :]] * (WIDE // 128), axis=1)
            kt_ref[mine, here] = jnp.exp(sqe[0:1, here] + left + inner * (2.0 * width_factor / features)).astype(jnp.bfloat16)

    for wave in (0, 1):
        for p in range(3 * wave, 3 * wave + 3):
            spread.pair_back(p)
        form(spread.mine + wave * (n // 4), n // 4)
    for p in P:
        spread.arrived(p)
    form(spread.other, n // 2)

    def upper(c):
        part = lax.dot_general(kt_ref[:c + 256, :], kt_ref[c:c + 256, :], (((1,), (1,)), ((), ())), preferred_element_type=jnp.float32)
        for j in (c // 128, c // 128 + 1):
            to = GRAM_AT[j]
            parts[to:to + c + 256, :] = part[:, j * 128 - c:j * 128 - c + 128]

    upper(768)
    add.pair(0)
    upper(512)
    part = jnp.dot(kt_ref[...], res[...].astype(jnp.bfloat16), preferred_element_type=jnp.float32) - shift_ref[...]
    for h, to in enumerate(GRAD_AT):
        parts[to:to + n, :] = part[:, h * 128:h * 128 + 128]
    for p in (1, 2, 3):
        add.pair(p)
    upper(256)
    add.pair(4)
    upper(0)
    add.pair(5)
    for p in P:
        add.scatter1(p)
    for name in STEPS[1:]:
        for p in P:
            getattr(add, name)(p)
    for p in P:
        add.arrived(p)
    for copy in sent:
        copy.wait_send()

def sum_scratch(rows, columns, dt):
    half = rows // 2
    return [pltpu.VMEM((half, columns), dt), pltpu.VMEM((half, columns), dt),
            pltpu.VMEM((3, half // 4, columns), dt), pltpu.VMEM((3, half // 16, columns), dt), pltpu.VMEM((3, half // 16, columns), dt),
            pltpu.SemaphoreType.DMA((2, 6, 2)), pltpu.SemaphoreType.DMA((5, 6, 3, 2))]

def sums_and_kernel(kept, examples, residuals, shift):
    n, features = kept.shape
    count, outputs = residuals.shape
    f32, bf16 = jnp.float32, jnp.bfloat16
    vmem, any_ = pl.BlockSpec(memory_space=pltpu.VMEM), pl.BlockSpec(memory_space=pl.ANY)
    return pl.pallas_call(
        step_kernel,
        out_shape=(jax.ShapeDtypeStruct((n, count), bf16), jax.ShapeDtypeStruct((2 * HALF, 128), f32)),
        in_specs=[vmem, any_, any_, vmem],
        out_specs=[vmem, vmem],
        scratch_shapes=[pltpu.VMEM((n, features), bf16)] + sum_scratch(n, features, bf16)
        + [pltpu.VMEM((2 * HALF, 128), f32)] + sum_scratch(2 * HALF, 128, f32)
        + [pltpu.VMEM((count, features), bf16), pltpu.VMEM((count, outputs), f32), pltpu.VMEM((n, 128), f32), pltpu.VMEM((8, count), f32),
           pltpu.SemaphoreType.DMA((2,))],
        compiler_params=pltpu.CompilerParams(collective_id=1, has_side_effects=True, vmem_limit_bytes=42 * 2**20),
        name="spread_and_sum",
    )(kept, examples, residuals, shift)


def split3(v):
    h = v.astype(jnp.bfloat16).astype(jnp.float32)
    r = v - h
    m = r.astype(jnp.bfloat16).astype(jnp.float32)
    return h, m, r - m

def stacks(v, axis):
    h, m, l = [x.astype(jnp.bfloat16) for x in split3(v)]
    return jnp.concatenate([h, h, m, h, m, l], axis=axis), jnp.concatenate([h, m, h, l, m, h], axis=axis)

def left(v, axis):
    return stacks(v, axis)[0]

def right(v, axis):
    return stacks(v, axis)[1]

def dot(a, b, ca, cb):
    return lax.dot_general(a, b, (((ca,), (cb,)), ((), ())), preferred_element_type=jnp.float32)

def factor(M, tasks=()):
    done = 0
    sub = lax.broadcasted_iota(jnp.int32, (8, 128), 0)
    sub2 = lax.broadcasted_iota(jnp.int32, (8, 256), 0)
    lane = lax.broadcasted_iota(jnp.int32, (8, 128), 1)

    def columns(v, first):
        return [jnp.broadcast_to(v[:, first + j:first + j + 1], (8, 128)) for j in range(8)]

    top = M[0:8, :]
    own = columns(top, 0)
    bot = M[8:16, :]
    for q in range(16):
        r0 = 8 * q
        look = q < 15
        if look:
            own = own + columns(top, r0 + 8)
            below = columns(bot, r0) + columns(bot, r0 + 8)
        if q < 14:
            far = M[r0 + 16:r0 + 24, :]
            beyond = columns(far, r0)
        for j in range(8):
            r = lax.rsqrt(own[j][j:j + 1, :])
            r2 = jnp.concatenate([r, r], axis=1)
            row = top[j:j + 1, :] * r2
            mt = jnp.where(sub > j, own[j] * r, 0.0)
            mt2 = jnp.concatenate([mt, mt], axis=1)
            steps = {k: own[k][j:j + 1, :] * r for k in range(j + 1, len(own))}
            top = jnp.where(sub2 == j, row, top - mt2 * row)
            for k in steps:
                own[k] = own[k] - mt * steps[k]
            if look:
                mb = below[j] * r
                mb2 = jnp.concatenate([mb, mb], axis=1)
                bot = bot - mb2 * row
                for k in steps:
                    below[k] = below[k] - mb * steps[k]
            if q < 14:
                mf = beyond[j] * r
                far = far - jnp.concatenate([mf, mf], axis=1) * row
                for k in range(j + 1, 8):
                    beyond[k] = beyond[k] - mf * steps[k]
        M[r0:r0 + 8, :] = top
        if q < 13:
            h, m, l = split3(top)
            keep = lane >= r0 + 24
            hl, ml, ll = [jnp.where(keep, v[:, :128], 0.0) for v in (h, m, l)]
            lhs = jnp.concatenate([hl, hl, ml, hl, ml, ll], axis=0).astype(jnp.bfloat16)
            rhs = jnp.concatenate([h, m, h, l, m, h], axis=0).astype(jnp.bfloat16)
            res = dot(lhs, rhs, 0, 0)
            M[r0 + 24:, :] = M[r0 + 24:, :] - res[r0 + 24:, :]
        if look:
            top, own = bot, below[8:]
        if q < 14:
            bot = far
        until = len(tasks) * (q + 1) // 14 if q < 13 else len(tasks)
        for task in tasks[done:until]:
            task()
        done = max(done, until)

def solve_kernel(scale, ridge, sums_ref, upd_ref, low_ref, S, G, M, V, UL, UR):
    n = S.shape[0]
    nb = n // NB
    eye = (lax.broadcasted_iota(jnp.int32, (NB, NB), 0) == lax.broadcasted_iota(jnp.int32, (NB, NB), 1)).astype(jnp.float32)
    for j, to in enumerate(GRAM_AT):
        S[0:depth_of(j), j * NB:j * NB + NB] = sums_ref[to:to + depth_of(j), :] * scale
    for j, to in enumerate(GRAD_AT):
        G[:, j * NB:j * NB + NB] = sums_ref[to:to + n, :] * scale

    def after(k, w):
        a, b = k * NB, (k + 1) * NB
        wl = left(w, 1)
        made = {}

        def keep(lo, hi):
            u = dot(wl, right(S[a:b, lo:hi], 0), 1, 0)
            S[a:b, lo:hi] = u
            UL[:, lo:hi], UR[:, lo:hi] = stacks(u, 0)

        def row(i, lo, hi):
            S[i:i + NB, lo:hi] = S[i:i + NB, lo:hi] - dot(UL[:, i:i + NB], UR[:, lo:hi], 0, 0)

        def forward():
            y = dot(wl, right(G[a:b, :], 0), 1, 0)
            G[a:b, :] = y
            made["y"] = right(y, 0)
            made["w"] = left(w, 0)

        def lower(i):
            G[i:i + NB, :] = G[i:i + NB, :] - dot(UL[:, i:i + NB], made["y"], 0, 0)

        def back():
            G[a:b, :] = dot(made["w"], made["y"], 0, 0)
            if b < n:
                V[a:b, b:] = dot(made["w"], UR[:, b:], 0, 0)

        tasks = []
        if b < n:
            c = b + NB
            keep(b, c)
            row(b, b, c)
            if c < n:
                tasks.append(lambda: keep(c, n))
                tasks.append(lambda: row(b, c, n))
        tasks.append(forward)
        for i in range(b, n, NB):
            if i > b:
                tasks.append(functools.partial(row, i, i, n))
            tasks.append(functools.partial(lower, i))
        tasks.append(back)
        return tasks

    tasks = []
    for k in range(nb):
        a, b = k * NB, (k + 1) * NB
        M[:, :NB] = S[a:b, a:b] + ridge * eye
        M[:, NB:] = eye
        factor(M, tasks)
        tasks = after(k, M[:, NB:])
    for task in tasks:
        task()
    for j in range(n - NB, 0, -NB):
        x = right(G[j:j + NB, :], 0)
        for i in range(j - NB, -1, -NB):
            G[i:i + NB, :] = G[i:i + NB, :] - dot(left(V[i:i + NB, j:j + NB], 1), x, 1, 0)
    upd_ref[...] = G[...]
    low_ref[...] = G[...].astype(jnp.bfloat16)

def solve(sums, n, o, total, ridge):
    return pl.pallas_call(
        functools.partial(solve_kernel, 1.0 / total, ridge),
        out_shape=(jax.ShapeDtypeStruct((n, o), jnp.float32), jax.ShapeDtypeStruct((n, o), jnp.bfloat16)),
        in_specs=[pl.BlockSpec(memory_space=pltpu.VMEM)],
        out_specs=[pl.BlockSpec(memory_space=pltpu.VMEM)] * 2,
        scratch_shapes=[pltpu.VMEM((n, n), jnp.float32), pltpu.VMEM((n, o), jnp.float32), pltpu.VMEM((NB, 2 * NB), jnp.float32), pltpu.VMEM((n, n), jnp.float32), pltpu.VMEM((6 * NB, n), jnp.bfloat16), pltpu.VMEM((6 * NB, n), jnp.bfloat16)],
        compiler_params=pltpu.CompilerParams(vmem_limit_bytes=32 * 2**20),
        name="solve_block",
    )(sums)


def body(examples, residuals, coefficients, block_index):
    rows_here = examples.shape[0]
    per_device = rows_here // BLOCK
    devices_all = lax.axis_size(("row", "col"))
    total_examples = rows_here * devices_all
    chosen = block_index[0]
    owner_rank = chosen // per_device
    offset = chosen % per_device * BLOCK
    my_rank = lax.axis_index(("row", "col"))
    is_owner = owner_rank == my_rank
    my_block = lax.dynamic_slice_in_dim(examples, offset, BLOCK, 0)
    kept = jnp.where(is_owner, my_block, 0).astype(my_block.dtype)
    own_coef = lax.dynamic_slice_in_dim(coefficients, offset, BLOCK, 0)
    weight_own = jnp.where(is_owner, total_examples * ridge, 0.0).astype(jnp.float32)
    kernel_t, sums = sums_and_kernel(kept, examples, residuals, weight_own * own_coef)
    update, update_low = solve(sums, BLOCK, own_coef.shape[1], total_examples, ridge)
    change = lax.dot_general(kernel_t, update_low, (((0,), (0,)), ((), ())), preferred_element_type=jnp.float32)
    new_residuals = residuals - change
    updated = lax.dynamic_update_slice_in_dim(coefficients, own_coef + update, offset, 0)
    new_coefficients = jnp.where(is_owner, updated, coefficients)
    return (new_residuals, new_coefficients)


def solution(mesh):
    in_specs = (P(("row", "col"), None), P(("row", "col"), None), P(("row", "col"), None), P())
    out_specs = (P(("row", "col"), None), P(("row", "col"), None))
    return jax.shard_map(body, mesh=mesh, in_specs=in_specs, out_specs=out_specs, check_vma=False)
```

```python
import functools
import jax
import jax.numpy as jnp
from jax import lax
from jax.experimental import pallas as pl
from jax.experimental.pallas import tpu as pltpu
from jax.sharding import PartitionSpec as P

BLOCK = 1024

ridge = 0.001
width_factor = 0.5


BLOCK_PARTS = tuple((r, 256, c, n) for r in (0, 256) for c, n in ((0, 384), (384, 384), (768, 256)))
SUM_PARTS = tuple((r, n, 0, 128) for r, n in ((0, 640), (640, 640), (1280, 512), (1792, 640), (2432, 640), (3072, 512)))
AXES = ("x", "y", "z")
NB = 128
CHUNK = 256
WIDE = 512
HALF = 3584
GRAM_AT = (HALF + 3072, HALF + 3328, HALF + 2560, 3072, HALF + 1024, HALF + 1792, 0, HALF)
GRAD_AT = (1024, 2048)

def depth_of(j):
    return (j // 2 + 1) * 256

def place():
    row, col = lax.axis_index("row"), lax.axis_index("col")
    return {"x": (col // 2) % 2 * 2 + row // 4, "y": col // 4, "z": row % 4, "core": col % 2}

def device(at):
    return (at["x"] % 2 * 4 + at["z"], at["y"] * 4 + at["x"] // 2 * 2 + at["core"])

def shifted(at, axis, by):
    size = 2 if axis == "core" else 4
    return device({**at, axis: (at[axis] + by) % size})

class Sum:
    def __init__(self, at, parts, unit, x, out, theirs, acc, slot1, slot2, slot3, core_sems, ring_sems, sent):
        self.__dict__.update(locals())
        half = x.shape[0] // 2
        self.mine, self.other = at["core"] * half, (1 - at["core"]) * half
        self.orders = [tuple(AXES[(p + i) % 3] for i in range(3)) for p in range(len(parts))]
        self.wait, self.begin, self.fine = {}, {}, {}

    def rows(self, start, n, c0, cn):
        return (pl.ds(pl.multiple_of(start, self.unit), n), pl.ds(c0, cn))

    def send(self, src, dst, sems, who):
        copy = pltpu.make_async_remote_copy(src_ref=src, dst_ref=dst, send_sem=sems.at[0], recv_sem=sems.at[1],
                                            device_id=who, device_id_type=pl.DeviceIdType.MESH)
        copy.start()
        self.sent.append(copy)
        return copy

    def arrived(self, p):
        for copy in self.wait[p]:
            copy.wait_recv()
        return self.parts[p]

    def to_peers(self, p, axis, stage, piece):
        self.wait[p] = [self.send(*piece(o), self.ring_sems.at[stage, p, o - 1], shifted(self.at, axis, o)) for o in (1, 2, 3)]

    def total(self, own, slot, where):
        sl = lambda o: slot[(o - 1,) + where]
        return (self.acc[own] + sl(2)) + (sl(1) + sl(3))

    def pair(self, p):
        r, n, c0, cn = self.parts[p]
        self.wait[p] = [self.send(self.x.at[self.rows(self.other + r, n, c0, cn)], self.theirs.at[self.rows(r, n, c0, cn)],
                                  self.core_sems.at[0, p], shifted(self.at, "core", 1))]

    def scatter1(self, p):
        r, n, c0, cn = self.arrived(p)
        self.acc[self.rows(r, n, c0, cn)] = self.x[self.rows(self.mine + r, n, c0, cn)] + self.theirs[self.rows(r, n, c0, cn)]
        q, a = n // 4, self.orders[p][0]
        self.to_peers(p, a, 0, lambda o: (self.acc.at[self.rows(r + (self.at[a] + o) % 4 * q, q, c0, cn)],
                                          self.slot1.at[o - 1, pl.ds(r // 4, q), pl.ds(c0, cn)]))

    def scatter2(self, p):
        r, n, c0, cn = self.arrived(p)
        q, s = n // 4, n // 16
        a, b = self.orders[p][:2]
        start = self.begin[p] = r + self.at[a] * q
        own = self.rows(start, q, c0, cn)
        self.acc[own] = self.total(own, self.slot1, (pl.ds(r // 4, q), pl.ds(c0, cn)))
        self.to_peers(p, b, 1, lambda o: (self.acc.at[self.rows(start + (self.at[b] + o) % 4 * s, s, c0, cn)],
                                          self.slot2.at[o - 1, pl.ds(r // 16, s), pl.ds(c0, cn)]))

    def exchange(self, p):
        r, n, c0, cn = self.arrived(p)
        s = n // 16
        b, d = self.orders[p][1:]
        start = self.fine[p] = self.begin[p] + self.at[b] * s
        own = self.rows(start, s, c0, cn)
        self.acc[own] = self.total(own, self.slot2, (pl.ds(r // 16, s), pl.ds(c0, cn)))
        self.to_peers(p, d, 2, lambda o: (self.acc.at[own], self.slot3.at[o - 1, pl.ds(r // 16, s), pl.ds(c0, cn)]))

    def gather2(self, p):
        r, n, c0, cn = self.arrived(p)
        s = n // 16
        here = self.rows(self.mine + self.fine[p], s, c0, cn)
        self.out[here] = self.total(self.rows(self.fine[p], s, c0, cn), self.slot3, (pl.ds(r // 16, s), pl.ds(c0, cn)))
        self.to_peers(p, self.orders[p][1], 3, lambda o: (self.out.at[here],) * 2)

    def gather1(self, p):
        r, n, c0, cn = self.arrived(p)
        here = self.rows(self.mine + self.begin[p], n // 4, c0, cn)
        self.to_peers(p, self.orders[p][0], 4, lambda o: (self.out.at[here],) * 2)

    def pair_back(self, p):
        r, n, c0, cn = self.arrived(p)
        here = self.out.at[self.rows(self.mine + r, n, c0, cn)]
        self.wait[p] = [self.send(here, here, self.core_sems.at[1, p], shifted(self.at, "core", 1))]

STEPS = ("scatter1", "scatter2", "exchange", "gather2", "gather1", "pair_back")

def step_kernel(x_ref, examples_ref, residuals_ref, shift_ref, kt_ref, sums_ref,
                block, theirs_b, acc_b, slot1_b, slot2_b, slot3_b, core_b, ring_b,
                parts, theirs_s, acc_s, slot1_s, slot2_s, slot3_s, core_s, ring_s,
                ex, res, sqb, sqe, load_sems):
    at = place()
    n, features = block.shape
    count = ex.shape[0]
    barrier = pltpu.get_barrier_semaphore()
    peers = [("core", 1)] + [(a, o) for a in AXES for o in (1, 2, 3)]
    for axis, by in peers:
        pl.semaphore_signal(barrier, inc=1, device_id=shifted(at, axis, by), device_id_type=pl.DeviceIdType.MESH)
    loads = [pltpu.make_async_copy(examples_ref, ex, load_sems.at[0]), pltpu.make_async_copy(residuals_ref, res, load_sems.at[1])]
    for load in loads:
        load.start()
    pl.semaphore_wait(barrier, len(peers))
    sent = []
    spread = Sum(at, BLOCK_PARTS, 16, x_ref, block, theirs_b, acc_b, slot1_b, slot2_b, slot3_b, core_b, ring_b, sent)
    add = Sum(at, SUM_PARTS, 8, parts, sums_ref, theirs_s, acc_s, slot1_s, slot2_s, slot3_s, core_s, ring_s, sent)
    P = range(6)
    for p in P:
        spread.pair(p)
    for p in P:
        spread.scatter1(p)
    loads[0].wait()

    def squares(first, last):
        @pl.loop(first, last)
        def _(i):
            here = pl.ds(pl.multiple_of(i * CHUNK, CHUNK), CHUNK)
            total = jnp.zeros((CHUNK, 128), jnp.float32)
            for f in range(0, features, 128):
                e = ex[here, f:f + 128].astype(jnp.float32)
                total = total + e * e
            high = total.astype(jnp.bfloat16)
            rest = total - high.astype(jnp.float32)
            middle = rest.astype(jnp.bfloat16)
            low = (rest - middle.astype(jnp.float32)).astype(jnp.bfloat16)
            sqe[:, here] = lax.dot_general(jnp.full((16, 384), 1.0, jnp.bfloat16), jnp.concatenate([high, middle, low], axis=1),
                                           (((1,), (1,)), ((), ())), preferred_element_type=jnp.float32)[:8, :] * (-width_factor / features)

    steps = count // CHUNK
    squares(0, steps // 2)
    for name in STEPS[1:-1]:
        for p in P:
            getattr(spread, name)(p)
        if name == "scatter2":
            squares(steps // 2, steps)
            loads[1].wait()

    def form(start, rows):
        mine = pl.ds(pl.multiple_of(start, rows), rows)
        b = block[mine, :].astype(jnp.float32)
        sqb[mine, :] = jnp.broadcast_to(jnp.sum(b * b, axis=1, keepdims=True) * (-width_factor / features), (rows, 128))

        @pl.loop(0, count // WIDE, unroll=2)
        def _(i):
            here = pl.ds(pl.multiple_of(i * WIDE, WIDE), WIDE)
            inner = lax.dot_general(block[mine, :], ex[here, :], (((1,), (1,)), ((), ())), preferred_element_type=jnp.float32)
            left = jnp.concatenate([sqb[mine, :]] * (WIDE // 128), axis=1)
            kt_ref[mine, here] = jnp.exp(sqe[0:1, here] + left + inner * (2.0 * width_factor / features)).astype(jnp.bfloat16)

    for wave in (0, 1):
        for p in range(3 * wave, 3 * wave + 3):
            spread.pair_back(p)
        form(spread.mine + wave * (n // 4), n // 4)
    for p in P:
        spread.arrived(p)
    form(spread.other, n // 2)

    def upper(c):
        part = lax.dot_general(kt_ref[:c + 256, :], kt_ref[c:c + 256, :], (((1,), (1,)), ((), ())), preferred_element_type=jnp.float32)
        for j in (c // 128, c // 128 + 1):
            to = GRAM_AT[j]
            parts[to:to + c + 256, :] = part[:, j * 128 - c:j * 128 - c + 128]

    upper(768)
    add.pair(0)
    upper(512)
    part = jnp.dot(kt_ref[...], res[...].astype(jnp.bfloat16), preferred_element_type=jnp.float32) - shift_ref[...]
    for h, to in enumerate(GRAD_AT):
        parts[to:to + n, :] = part[:, h * 128:h * 128 + 128]
    for p in (1, 2, 3):
        add.pair(p)
    upper(256)
    add.pair(4)
    upper(0)
    add.pair(5)
    for p in P:
        add.scatter1(p)
    for name in STEPS[1:]:
        for p in P:
            getattr(add, name)(p)
    for p in P:
        add.arrived(p)
    for copy in sent:
        copy.wait_send()

def sum_scratch(rows, columns, dt):
    half = rows // 2
    return [pltpu.VMEM((half, columns), dt), pltpu.VMEM((half, columns), dt),
            pltpu.VMEM((3, half // 4, columns), dt), pltpu.VMEM((3, half // 16, columns), dt), pltpu.VMEM((3, half // 16, columns), dt),
            pltpu.SemaphoreType.DMA((2, 6, 2)), pltpu.SemaphoreType.DMA((5, 6, 3, 2))]

def sums_and_kernel(kept, examples, residuals, shift):
    n, features = kept.shape
    count, outputs = residuals.shape
    f32, bf16 = jnp.float32, jnp.bfloat16
    vmem, any_ = pl.BlockSpec(memory_space=pltpu.VMEM), pl.BlockSpec(memory_space=pl.ANY)
    return pl.pallas_call(
        step_kernel,
        out_shape=(jax.ShapeDtypeStruct((n, count), bf16), jax.ShapeDtypeStruct((2 * HALF, 128), f32)),
        in_specs=[vmem, any_, any_, vmem],
        out_specs=[vmem, vmem],
        scratch_shapes=[pltpu.VMEM((n, features), bf16)] + sum_scratch(n, features, bf16)
        + [pltpu.VMEM((2 * HALF, 128), f32)] + sum_scratch(2 * HALF, 128, f32)
        + [pltpu.VMEM((count, features), bf16), pltpu.VMEM((count, outputs), f32), pltpu.VMEM((n, 128), f32), pltpu.VMEM((8, count), f32),
           pltpu.SemaphoreType.DMA((2,))],
        compiler_params=pltpu.CompilerParams(collective_id=1, has_side_effects=True, vmem_limit_bytes=34 * 2**20),
        name="spread_and_sum",
    )(kept, examples, residuals, shift)


def split3(v):
    h = v.astype(jnp.bfloat16).astype(jnp.float32)
    r = v - h
    m = r.astype(jnp.bfloat16).astype(jnp.float32)
    return h, m, r - m

def stacks(v, axis):
    h, m, l = [x.astype(jnp.bfloat16) for x in split3(v)]
    return jnp.concatenate([h, h, m, h, m, l], axis=axis), jnp.concatenate([h, m, h, l, m, h], axis=axis)

def left(v, axis):
    return stacks(v, axis)[0]

def right(v, axis):
    return stacks(v, axis)[1]

def dot(a, b, ca, cb):
    return lax.dot_general(a, b, (((ca,), (cb,)), ((), ())), preferred_element_type=jnp.float32)

def factor(M, tasks=()):
    done = 0
    sub = lax.broadcasted_iota(jnp.int32, (8, 128), 0)
    sub2 = lax.broadcasted_iota(jnp.int32, (8, 256), 0)
    lane = lax.broadcasted_iota(jnp.int32, (8, 128), 1)

    def columns(v, first):
        return [jnp.broadcast_to(v[:, first + j:first + j + 1], (8, 128)) for j in range(8)]

    top = M[0:8, :]
    own = columns(top, 0)
    bot = M[8:16, :]
    for q in range(16):
        r0 = 8 * q
        look = q < 15
        if look:
            own = own + columns(top, r0 + 8)
            below = columns(bot, r0) + columns(bot, r0 + 8)
        if q < 14:
            far = M[r0 + 16:r0 + 24, :]
            beyond = columns(far, r0)
        for j in range(8):
            r = lax.rsqrt(own[j][j:j + 1, :])
            r2 = jnp.concatenate([r, r], axis=1)
            row = top[j:j + 1, :] * r2
            mt = jnp.where(sub > j, own[j] * r, 0.0)
            mt2 = jnp.concatenate([mt, mt], axis=1)
            steps = {k: own[k][j:j + 1, :] * r for k in range(j + 1, len(own))}
            top = jnp.where(sub2 == j, row, top - mt2 * row)
            for k in steps:
                own[k] = own[k] - mt * steps[k]
            if look:
                mb = below[j] * r
                mb2 = jnp.concatenate([mb, mb], axis=1)
                bot = bot - mb2 * row
                for k in steps:
                    below[k] = below[k] - mb * steps[k]
            if q < 14:
                mf = beyond[j] * r
                far = far - jnp.concatenate([mf, mf], axis=1) * row
                for k in range(j + 1, 8):
                    beyond[k] = beyond[k] - mf * steps[k]
        M[r0:r0 + 8, :] = top
        if q < 13:
            h, m, l = split3(top)
            keep = lane >= r0 + 24
            hl, ml, ll = [jnp.where(keep, v[:, :128], 0.0) for v in (h, m, l)]
            lhs = jnp.concatenate([hl, hl, ml, hl, ml, ll], axis=0).astype(jnp.bfloat16)
            rhs = jnp.concatenate([h, m, h, l, m, h], axis=0).astype(jnp.bfloat16)
            res = dot(lhs, rhs, 0, 0)
            M[r0 + 24:, :] = M[r0 + 24:, :] - res[r0 + 24:, :]
        if look:
            top, own = bot, below[8:]
        if q < 14:
            bot = far
        until = len(tasks) * (q + 1) // 14 if q < 13 else len(tasks)
        for task in tasks[done:until]:
            task()
        done = max(done, until)

def solve_kernel(scale, ridge, sums_ref, upd_ref, low_ref, S, G, M, V, UL, UR):
    n = S.shape[0]
    nb = n // NB
    eye = (lax.broadcasted_iota(jnp.int32, (NB, NB), 0) == lax.broadcasted_iota(jnp.int32, (NB, NB), 1)).astype(jnp.float32)
    for j, to in enumerate(GRAM_AT):
        S[0:depth_of(j), j * NB:j * NB + NB] = sums_ref[to:to + depth_of(j), :] * scale
    for j, to in enumerate(GRAD_AT):
        G[:, j * NB:j * NB + NB] = sums_ref[to:to + n, :] * scale

    def after(k, w):
        a, b = k * NB, (k + 1) * NB
        wl = left(w, 1)
        made = {}

        def keep(lo, hi):
            u = dot(wl, right(S[a:b, lo:hi], 0), 1, 0)
            S[a:b, lo:hi] = u
            UL[:, lo:hi], UR[:, lo:hi] = stacks(u, 0)

        def row(i, lo, hi):
            S[i:i + NB, lo:hi] = S[i:i + NB, lo:hi] - dot(UL[:, i:i + NB], UR[:, lo:hi], 0, 0)

        def forward():
            y = dot(wl, right(G[a:b, :], 0), 1, 0)
            G[a:b, :] = y
            made["y"] = right(y, 0)
            made["w"] = left(w, 0)

        def lower(i):
            G[i:i + NB, :] = G[i:i + NB, :] - dot(UL[:, i:i + NB], made["y"], 0, 0)

        def back():
            G[a:b, :] = dot(made["w"], made["y"], 0, 0)
            if b < n:
                V[a:b, b:] = dot(made["w"], UR[:, b:], 0, 0)

        tasks = []
        if b < n:
            c = b + NB
            keep(b, c)
            row(b, b, c)
            if c < n:
                tasks.append(lambda: keep(c, n))
                tasks.append(lambda: row(b, c, n))
        tasks.append(forward)
        for i in range(b, n, NB):
            if i > b:
                tasks.append(functools.partial(row, i, i, n))
            tasks.append(functools.partial(lower, i))
        tasks.append(back)
        return tasks

    tasks = []
    for k in range(nb):
        a, b = k * NB, (k + 1) * NB
        M[:, :NB] = S[a:b, a:b] + ridge * eye
        M[:, NB:] = eye
        factor(M, tasks)
        tasks = after(k, M[:, NB:])
    for task in tasks:
        task()
    for j in range(n - NB, 0, -NB):
        x = right(G[j:j + NB, :], 0)
        for i in range(j - NB, -1, -NB):
            G[i:i + NB, :] = G[i:i + NB, :] - dot(left(V[i:i + NB, j:j + NB], 1), x, 1, 0)
    upd_ref[...] = G[...]
    low_ref[...] = G[...].astype(jnp.bfloat16)

def solve(sums, n, o, total, ridge):
    return pl.pallas_call(
        functools.partial(solve_kernel, 1.0 / total, ridge),
        out_shape=(jax.ShapeDtypeStruct((n, o), jnp.float32), jax.ShapeDtypeStruct((n, o), jnp.bfloat16)),
        in_specs=[pl.BlockSpec(memory_space=pltpu.VMEM)],
        out_specs=[pl.BlockSpec(memory_space=pltpu.VMEM)] * 2,
        scratch_shapes=[pltpu.VMEM((n, n), jnp.float32), pltpu.VMEM((n, o), jnp.float32), pltpu.VMEM((NB, 2 * NB), jnp.float32), pltpu.VMEM((n, n), jnp.float32), pltpu.VMEM((6 * NB, n), jnp.bfloat16), pltpu.VMEM((6 * NB, n), jnp.bfloat16)],
        compiler_params=pltpu.CompilerParams(vmem_limit_bytes=32 * 2**20),
        name="solve_block",
    )(sums)


def body(examples, residuals, coefficients, block_index):
    rows_here = examples.shape[0]
    per_device = rows_here // BLOCK
    devices_all = lax.axis_size(("row", "col"))
    total_examples = rows_here * devices_all
    chosen = block_index[0]
    owner_rank = chosen // per_device
    offset = chosen % per_device * BLOCK
    my_rank = lax.axis_index(("row", "col"))
    is_owner = owner_rank == my_rank
    my_block = lax.dynamic_slice_in_dim(examples, offset, BLOCK, 0)
    kept = jnp.where(is_owner, my_block, 0).astype(my_block.dtype)
    own_coef = lax.dynamic_slice_in_dim(coefficients, offset, BLOCK, 0)
    weight_own = jnp.where(is_owner, total_examples * ridge, 0.0).astype(jnp.float32)
    kernel_t, sums = sums_and_kernel(kept, examples, residuals, weight_own * own_coef)
    update, update_low = solve(sums, BLOCK, own_coef.shape[1], total_examples, ridge)
    change = lax.dot_general(kernel_t, update_low, (((0,), (0,)), ((), ())), preferred_element_type=jnp.float32)
    new_residuals = residuals - change
    updated = lax.dynamic_update_slice_in_dim(coefficients, own_coef + update, offset, 0)
    new_coefficients = jnp.where(is_owner, updated, coefficients)
    return (new_residuals, new_coefficients)


def solution(mesh):
    in_specs = (P(("row", "col"), None), P(("row", "col"), None), P(("row", "col"), None), P())
    out_specs = (P(("row", "col"), None), P(("row", "col"), None))
    return jax.shard_map(body, mesh=mesh, in_specs=in_specs, out_specs=out_specs, check_vma=False)
```
